32 devices in a mesh: rows: 16 (over z, y, core), chan: 2 (over x).
Axes of the slice: x: 2, y: 2, z: 4, core: 2. Of those that a mesh axis runs over, the one named last changes fastest.
Arguments:
- features: bfloat16 [64, 128, 2048], P('rows', None, 'chan'), may hold values from 0 to 12, as said below
- low_features: bfloat16 [256, 512, 256], P('rows', 'chan'), may hold values from -6 to 6
- w_one: bfloat16 [2048, 256], P('chan'), may hold values from -0.125 to 0.125
- w_rate: bfloat16 [3, 9, 2048, 256], P(None, None, 'chan', 'rows'), may hold values from -0.046875 to 0.046875
- w_pool: bfloat16 [2048, 256], P('chan'), may hold values from -0.125 to 0.125
- b_branch: float32 [5, 256], replicated, may hold values from -3 to 3
- w_proj: bfloat16 [1280, 256], replicated, may hold values from -0.15625 to 0.15625
- b_proj: float32 [256], replicated, may hold values from -3 to 3
- w_low: bfloat16 [256, 48], replicated, may hold values from -0.375 to 0.375
- b_low: float32 [48], replicated, may hold values from -3 to 3
- w_dec_up: bfloat16 [9, 256, 256], replicated, may hold values from -0.109375 to 0.109375
- w_dec_low: bfloat16 [9, 48, 256], replicated, may hold values from -0.109375 to 0.109375
- b_dec: float32 [256], replicated, may hold values from -3 to 3
Outputs:
- context: bfloat16 [64, 128, 256], P('rows', 'chan')
- decoded: bfloat16 [256, 512, 256], P('rows', 'chan')
The draws below stay inside these ranges and needn't reach their ends.
Inputs may be any that keep to these rules, and one draw needn't show every extreme that they name: features are nonnegative.
All inputs are finite; a program needn't handle non-finite values.
Results may differ from the reference program's by a relative error of at most 0.019.
Values may be sent and summed in bfloat16 or wider, within the bound.
A program may use at most 128 MiB of HBM per device.

```python
import math
import jax
import jax.numpy as jnp
from jax import lax

CIN = 2048
BR = 256
LOWC = 256
LOWP = 48
DEC = 256
RATE = 6
COLS = 128
GROUPS = 2
MAP_ROWS = 64
FINE_ROWS = 256
FINE_COLS = 512


def draw_features(key, part):
    keys = jax.random.split(jax.random.fold_in(key, 11), 4)
    shape = (MAP_ROWS, COLS, CIN)
    position = jnp.arange(MAP_ROWS, dtype=jnp.float32) / MAP_ROWS
    base = jnp.abs(jax.random.normal(keys[0], shape, jnp.float32))
    rising = 3.0 ** position
    row_spread = jnp.exp(jax.random.uniform(keys[1], (MAP_ROWS,), jnp.float32, 0.0, math.log(10.0)))
    col_scale = jnp.exp(jax.random.uniform(keys[2], (COLS,), jnp.float32, 0.0, math.log(10.0)))
    chan_scale = jnp.exp(jax.random.uniform(keys[3], (CIN,), jnp.float32, -math.log(2.0), math.log(2.0)))
    row_scale = rising * row_spread
    values = base * row_scale[:, None, None] * col_scale[None, :, None] * chan_scale[None, None, :] / 24.0
    return jnp.minimum(values, 12.0).astype(jnp.bfloat16)


def shard_levels(rng, extent, pieces, smallest, high):
    level, own = 1.0, jax.random.fold_in(rng, 6)
    for axis_at, blocks in pieces:
        steps = jnp.exp(jax.random.uniform(jax.random.fold_in(own, axis_at), (blocks,), jnp.float32, smallest / len(pieces), high / len(pieces)))
        level = level * jnp.repeat(steps, extent[axis_at] // blocks).reshape([-1 if axis == axis_at else 1 for axis in range(len(extent))])
    return level


def bell_draw(stream_key, shape, spread, limit, cuts=(), kind=jnp.bfloat16):
    entries = jax.random.normal(stream_key, shape, jnp.float32) * spread
    if len(cuts) > 0:
        entries = shard_levels(stream_key, shape, cuts, -0.22, 0.18) * entries
    return jnp.clip(entries, min=-limit, max=limit).astype(kind)


def setup_inputs(seed: int = 0) -> dict:
    key_list = jax.random.split(jax.random.key(seed), 14)
    return {
        "features": draw_features(jax.random.fold_in(key_list[13], 71), 0),
        "low_features": bell_draw(key_list[1], (FINE_ROWS, FINE_COLS, LOWC), 1.0, 6.0, ((0, 16), (1, 2))),
        "w_one": bell_draw(key_list[2], (CIN, BR), CIN ** -0.5, 0.125, ((0, 2),)),
        "w_rate": bell_draw(key_list[3], (3, 9, CIN, BR), (9 * CIN) ** -0.5, 0.046875, ((2, 2), (3, 16))),
        "w_pool": bell_draw(key_list[4], (CIN, BR), CIN ** -0.5, 0.125, ((0, 2),)),
        "b_branch": bell_draw(key_list[5], (5, BR), 0.5, 3.0, (), jnp.float32),
        "w_proj": bell_draw(key_list[6], (5 * BR, BR), (5 * BR) ** -0.5, 0.15625),
        "b_proj": bell_draw(key_list[7], (BR,), 0.5, 3.0, (), jnp.float32),
        "w_low": bell_draw(key_list[8], (LOWC, LOWP), LOWC ** -0.5, 0.375),
        "b_low": bell_draw(key_list[9], (LOWP,), 0.5, 3.0, (), jnp.float32),
        "w_dec_up": bell_draw(key_list[10], (9, BR, DEC), (9 * (BR + LOWP)) ** -0.5, 0.109375),
        "w_dec_low": bell_draw(key_list[11], (9, LOWP, DEC), (9 * (BR + LOWP)) ** -0.5, 0.109375),
        "b_dec": bell_draw(key_list[12], (DEC,), 0.5, 3.0, (), jnp.float32),
    }


BLEND = (0.875, 0.625, 0.375, 0.125)


def moved(field, down, across):
    count_rows = field.shape[0]
    count_cols = field.shape[1]
    pad_rows = abs(down)
    pad_cols = abs(across)
    padded = jnp.pad(field, ((pad_rows, pad_rows), (pad_cols, pad_cols), (0, 0)))
    return padded[pad_rows + down:pad_rows + down + count_rows, pad_cols + across:pad_cols + across + count_cols]


def blend_axis(field, axis_pos):
    count_in = field.shape[axis_pos]
    lower_half = lax.slice_in_dim(field, 0, count_in - 1, axis=axis_pos)
    upper_half = lax.slice_in_dim(field, 1, count_in, axis=axis_pos)
    blended = jnp.stack([factor * lower_half + (1.0 - factor) * upper_half for factor in BLEND], axis=axis_pos + 1)
    target = list(lower_half.shape)
    target[axis_pos] = 4 * (count_in - 1)
    return blended.reshape(target)


def reference(features, low_features, w_one, w_rate, w_pool, b_branch, w_proj, b_proj, w_low, b_low, w_dec_up, w_dec_low, b_dec):
    map_rows, map_cols, channels = features.shape
    branch_width = w_one.shape[1]
    group_in = channels // GROUPS
    pixel_count = map_rows * map_cols

    def add_group(total, first_in):
        part_in = lax.dynamic_slice_in_dim(features, first_in, group_in, 2)
        one_weight = lax.dynamic_slice_in_dim(w_one, first_in, group_in, 0)
        rate_weight = lax.dynamic_slice_in_dim(w_rate, first_in, group_in, 2)
        outputs = [jnp.dot(part_in.reshape(pixel_count, group_in), one_weight, preferred_element_type=jnp.float32)]
        for rate_level in range(3):
            spacing = RATE * (rate_level + 1)
            accum = jnp.zeros((pixel_count, branch_width), jnp.float32)
            for tap_index in range(9):
                down = (tap_index // 3 - 1) * spacing
                across = (tap_index % 3 - 1) * spacing
                source = moved(part_in, down, across).reshape(pixel_count, group_in)
                accum = accum + jnp.dot(source, rate_weight[rate_level, tap_index], preferred_element_type=jnp.float32)
            outputs.append(accum)
        partial_value = jnp.concatenate(outputs, axis=1).astype(jnp.bfloat16)
        partial_value = lax.optimization_barrier(partial_value)
        return total + partial_value.astype(jnp.float32), None

    starts = jnp.arange(GROUPS, dtype=jnp.int32) * group_in
    zeros = jnp.zeros((pixel_count, 4 * branch_width), jnp.float32)
    branch_sum, unused = lax.scan(add_group, zeros, starts)
    branches = jax.nn.relu(branch_sum + b_branch[:4].reshape(-1)).astype(jnp.bfloat16)

    pooled = jnp.sum(features.astype(jnp.float32), axis=(0, 1)) / pixel_count
    pool_pre = jnp.dot(pooled, w_pool.astype(jnp.float32), precision=lax.Precision.HIGHEST)
    pool_branch = jax.nn.relu(pool_pre + b_branch[4]).astype(jnp.bfloat16)
    pool_term = jnp.dot(pool_branch[None, :], w_proj[4 * branch_width:], preferred_element_type=jnp.float32)[0]
    projected = jnp.dot(branches, w_proj[:4 * branch_width], preferred_element_type=jnp.float32)
    context = jax.nn.relu(projected + pool_term + b_proj).astype(jnp.bfloat16).reshape(map_rows, map_cols, branch_width)

    fine_rows, fine_cols = low_features.shape[0], low_features.shape[1]
    low_flat = low_features.reshape(fine_rows * fine_cols, low_features.shape[2])
    low_mapped = jax.nn.relu(jnp.dot(low_flat, w_low, preferred_element_type=jnp.float32) + b_low).astype(jnp.bfloat16)
    low_mapped = low_mapped.reshape(fine_rows, fine_cols, -1)

    edged = jnp.pad(context.astype(jnp.float32), ((1, 1), (1, 1), (0, 0)), mode="edge")
    upsampled = blend_axis(edged, 0)[2:4 * map_rows + 2]
    upsampled = blend_axis(upsampled, 1)[:, 2:4 * map_cols + 2].astype(jnp.bfloat16)

    up_pad = jnp.pad(upsampled, ((1, 1), (1, 1), (0, 0)))
    low_pad = jnp.pad(low_mapped, ((1, 1), (1, 1), (0, 0)))
    accum = jnp.zeros((fine_rows * fine_cols, w_dec_up.shape[2]), jnp.float32)
    for tap_index in range(9):
        row_step = tap_index // 3
        col_step = tap_index % 3
        up_slice = up_pad[row_step:row_step + fine_rows, col_step:col_step + fine_cols].reshape(fine_rows * fine_cols, -1)
        low_slice = low_pad[row_step:row_step + fine_rows, col_step:col_step + fine_cols].reshape(fine_rows * fine_cols, -1)
        accum = accum + jnp.dot(up_slice, w_dec_up[tap_index], preferred_element_type=jnp.float32)
        accum = accum + jnp.dot(low_slice, w_dec_low[tap_index], preferred_element_type=jnp.float32)
    decoded = jax.nn.relu(accum + b_dec).astype(jnp.bfloat16).reshape(fine_rows, fine_cols, -1)
    return context, decoded
```

```python
import jax
import jax.numpy as jnp
from jax import lax
from jax.experimental import pallas as pl
from jax.experimental.pallas import tpu as pltpu
from jax.sharding import PartitionSpec as P

RATE = 6


BLEND = (0.875, 0.625, 0.375, 0.125)


def passed_along(block, axis, distance):
    devices = range(lax.axis_size(axis))
    route = [(i - distance, i) for i in devices if i - distance in devices]
    return lax.ppermute(block, axis, route)


def padded_2(array, sides, width):
    for axis, dim in sides:
        devices, length = (lax.axis_size(axis), array.shape[dim])
        up = [(i, (i + 1) % devices) for i in range(devices - 1)]
        down = [(j, i) for i, j in up]
        last = lax.slice_in_dim(array, length - width, length, axis=dim)
        first = lax.slice_in_dim(array, 0, width, axis=dim)
        before = lax.ppermute(last, axis, up)
        after = lax.ppermute(first, axis, down)
        array = jnp.concatenate([before, array, after], axis=dim)
    return array


def move_cols(field, across):
    extent = field.shape[1]
    amount = abs(across)
    padded = jnp.pad(field, ((0, 0), (amount, amount), (0, 0)))
    return padded[:, amount + across : amount + across + extent]


def fetch_rows(features, offset):
    hop_count, remain = divmod(offset, features.shape[0])
    upper_part = features[remain:]
    upper_part = passed_along(upper_part, "rows", -hop_count)
    if remain == 0:
        return upper_part
    lower_part = features[:remain]
    lower_part = passed_along(lower_part, "rows", -hop_count - 1)
    return jnp.concatenate([upper_part, lower_part], axis=0)


def rate_matrix(features, spacing):
    sources = (fetch_rows(features, -spacing), features, fetch_rows(features, spacing))
    pieces = [
        move_cols(source, (col_step - 1) * spacing) for source in sources for col_step in range(3)
    ]
    stacked = jnp.concatenate(pieces, axis=2)
    return stacked.reshape(-1, stacked.shape[2])


def blend_axis(field, axis_pos):
    count_in = field.shape[axis_pos]
    lower_half = lax.slice_in_dim(field, 0, count_in - 1, axis=axis_pos)
    upper_half = lax.slice_in_dim(field, 1, count_in, axis=axis_pos)
    blended = jnp.stack(
        [factor * lower_half + (1.0 - factor) * upper_half for factor in BLEND], axis=axis_pos + 1
    )
    target = list(lower_half.shape)
    target[axis_pos] = 4 * (count_in - 1)
    return blended.reshape(target)


def edge_copy(padded, rows_index, rows_count, chan_index, chan_count):
    top_row = jnp.where(rows_index == 0, padded[1:2], padded[0:1])
    bottom_row = jnp.where(rows_index == rows_count - 1, padded[-2:-1], padded[-1:])
    padded = jnp.concatenate([top_row, padded[1:-1], bottom_row], axis=0)
    left_col = jnp.where(chan_index == 0, padded[:, 1:2], padded[:, 0:1])
    right_col = jnp.where(chan_index == chan_count - 1, padded[:, -2:-1], padded[:, -1:])
    return jnp.concatenate([left_col, padded[:, 1:-1], right_col], axis=1)


def tap_matrix(padded, out_rows, out_cols):
    pieces = [
        padded[row_step : row_step + out_rows, col_step : col_step + out_cols]
        for row_step in range(3)
        for col_step in range(3)
    ]
    stacked = jnp.concatenate(pieces, axis=2)
    return stacked.reshape(out_rows * out_cols, -1)


F32 = jnp.float32
BF16 = jnp.bfloat16
MESH = pl.DeviceIdType.MESH


def dot_t(lhs, rhs):
    return lax.dot_general(lhs, rhs, (((1,), (1,)), ((), ())), preferred_element_type=F32)


def pyramid_kernel(
    geometry,
    f_ref, own_ref, one_ref, pool_ref, branch_bias_ref, proj_ref, proj_bias_ref,
    out_ref,
    wbuf, shifted, sums, row_send, row_recv, merged, chan_recv, total, context, halo,
    pool_send, pool_recv, pool_line,
    gather_send, gather_recv, row_ssem, row_rsem, chan_ssem, chan_rsem, halo_ssem, halo_rsem,
    pool_ssem, pool_rsem,
):
    rows, lines, window, fine = geometry
    strip, cols, depth = f_ref.shape
    width = one_ref.shape[1]
    pixels = strip * cols
    me = lax.axis_index("rows")
    chan = lax.axis_index("chan")
    mine_z = me // 4
    mine_y = (me // 2) % 2
    core_peer = me + 1 - 2 * (me % 2)
    y_peer = me + 2 - 4 * mine_y
    chan_peer = 1 - chan
    levels = own_ref.shape[0]
    pending = []

    def remote(src, dst, ssem, rsem, device):
        return pltpu.make_async_remote_copy(
            src_ref=src, dst_ref=dst, send_sem=ssem, recv_sem=rsem, device_id=device, device_id_type=MESH
        )

    def send(cond, copy):
        if cond is None:
            copy.start()
        else:
            pl.when(cond)(copy.start)
        pending.append((cond, copy))

    def arrive(cond, ref, rsem, ssem):
        copy = remote(ref, ref, ssem, rsem, {"chan": chan_peer})
        if cond is None:
            copy.wait_recv()
        else:
            pl.when(cond)(copy.wait_recv)

    row_recv[...] = jnp.zeros_like(row_recv)
    wbuf[me] = own_ref[...]

    barrier = pltpu.get_barrier_semaphore()
    for step in range(1, rows):
        pl.semaphore_signal(
            barrier, inc=1, device_id={"rows": lax.rem(me + step, rows)}, device_id_type=MESH
        )
    pl.semaphore_signal(barrier, inc=1, device_id={"chan": chan_peer}, device_id_type=MESH)
    pl.semaphore_wait(barrier, rows)

    counter = [0]

    def pass_shard(cond, source, level, target):
        index = counter[0]
        counter[0] += 1
        slot = wbuf.at[source, level]
        send(
            cond,
            remote(slot, slot, gather_send.at[index], gather_recv.at[level, source], {"rows": target}),
        )

    def shard_here(cond, source, level):
        arrive(cond, wbuf.at[source, level], gather_recv.at[level, source], gather_send.at[0])

    def both(one, other):
        return other if one is None else one & other

    order = list(range(levels))[::-1]
    for level in order:
        pass_shard(mine_z + 1 < lines, me, level, me + 4)
        pass_shard(mine_z > 0, me, level, me - 4)
        pass_shard(None, me, level, y_peer)
        pass_shard(None, me, level, core_peer)

    def flat():
        return f_ref[...].reshape(pixels, depth)

    local = jnp.zeros((8, depth), F32)
    for row in range(strip):
        block = f_ref[row].astype(F32).reshape(cols // 8, 8, depth)
        local = local + jnp.sum(block, axis=0)
    local = jnp.broadcast_to(jnp.sum(local, axis=0, keepdims=True), (8, depth))
    pool_send[0] = jnp.dot(
        local, pool_ref[...].astype(F32), precision=lax.Precision.HIGHEST, preferred_element_type=F32
    )
    peers = ({"chan": chan_peer}, {"rows": core_peer}, {"rows": y_peer})

    def pool_round(turn):
        send(
            None,
            remote(
                pool_send.at[turn], pool_recv.at[turn], pool_ssem.at[turn], pool_rsem.at[turn], peers[turn]
            ),
        )

    def pool_add(turn):
        arrive(None, pool_recv.at[turn], pool_rsem.at[turn], pool_ssem.at[turn])
        pool_send[turn + 1] = pool_send[turn] + pool_recv[turn]

    def merge(slot, value):
        merged[slot] = value.astype(BF16).reshape(strip, cols, width)
        start = pl.multiple_of(chan_peer * (cols - window), 16)
        send(
            None,
            remote(
                merged.at[slot, :, pl.ds(start, window), :],
                chan_recv.at[slot],
                chan_ssem.at[slot],
                chan_rsem.at[slot],
                {"chan": chan_peer},
            ),
        )

    def project(slot, first):
        arrive(None, chan_recv.at[slot], chan_rsem.at[slot], chan_ssem.at[slot])
        start = pl.multiple_of(chan * (cols - window), 16)
        value = merged[slot, :, pl.ds(start, window), :].astype(F32) + chan_recv[slot].astype(F32)
        value = jax.nn.relu(value + branch_bias_ref[slot : slot + 1, :].reshape(1, 1, width))
        value = value.astype(BF16).reshape(strip * window, width)
        term = jnp.dot(
            value, proj_ref[slot * width : (slot + 1) * width, :], preferred_element_type=F32
        )
        if first:
            total[...] = term
        else:
            total[...] += term

    def shift_level(level):
        spacing = RATE * (level + 1)
        pos = lax.broadcasted_iota(jnp.int32, (cols, depth), 0)
        for row in range(strip):
            value = f_ref[row].astype(F32)
            before = jnp.where(pos < spacing, 0.0, pltpu.roll(value, spacing, 0))
            after = jnp.where(pos >= cols - spacing, 0.0, pltpu.roll(value, cols - spacing, 0))
            shifted[level, 0, row] = before.astype(BF16)
            shifted[level, 1, row] = after.astype(BF16)

    pool_round(0)
    merge(0, jnp.dot(flat(), one_ref[...], preferred_element_type=F32))
    pool_add(0)
    pool_round(1)
    shift_level(order[0])
    pool_add(1)
    pool_round(2)
    for level in order[1:]:
        shift_level(level)
    pool_add(2)
    pool_line[mine_z] = pool_send[3]
    for step in range(1, lines):
        for at, sign in enumerate((1, -1)):
            there = mine_z + sign * step
            cond = (there >= 0) & (there < lines)
            send(
                cond,
                remote(
                    pool_send.at[3],
                    pool_line.at[mine_z],
                    pool_ssem.at[3 + 2 * (step - 1) + at],
                    pool_rsem.at[3 + mine_z],
                    {"rows": me + 4 * sign * step},
                ),
            )
    project(0, True)

    def gather_level(level):
        for step in range(1, lines):
            for sign in (-1, 1):
                source = me + 4 * sign * step
                here = (mine_z + sign * step >= 0) & (mine_z + sign * step < lines)
                beyond = here & (mine_z - sign >= 0) & (mine_z - sign < lines)
                shard_here(here, source, level)
                pass_shard(beyond, source, level, me - 4 * sign)
                pass_shard(here, source, level, y_peer)
                pass_shard(here, source, level, core_peer)
        for step in range(lines):
            for sign in (-1, 1) if step else (1,):
                source = y_peer + 4 * sign * step
                here = (mine_z + sign * step >= 0) & (mine_z + sign * step < lines)
                shard_here(here, source, level)
                pass_shard(here, source, level, core_peer)
        for line in range(lines):
            for y in range(2):
                shard_here(None, line * 4 + y * 2 + 1 - me % 2, level)

    def row_copies(level):
        hop, remain = divmod(RATE * (level + 1), strip)
        found = []
        if remain < strip:
            found.append((0, hop, 0, remain, strip - remain))
            found.append((1, -hop, remain, 0, strip - remain))
        if remain > 0:
            found.append((0, hop + 1, strip - remain, 0, remain))
            found.append((1, -hop - 1, 0, strip - remain, remain))
        return found

    def compute_level(level):
        spread = levels * 3

        @pl.loop(0, 3)
        def _(down):
            value = None
            for across in range(3):
                weight = wbuf[:, level, 3 * down + across].reshape(width, depth)
                side = f_ref[...] if across == 1 else shifted[level, across // 2]
                term = dot_t(side.reshape(pixels, depth), weight)
                value = term if value is None else value + term
            sums[level, down] = value

        for at, down in enumerate((0, 2)):
            row_send[level, at] = sums[level, down].astype(BF16).reshape(strip, cols, width)
        for index, (at, offset, first, into, count) in enumerate(row_copies(level)):
            cond = (me + offset >= 0) & (me + offset < rows)
            send(
                cond,
                remote(
                    row_send.at[level, at, pl.ds(first, count)],
                    row_recv.at[level, at, pl.ds(into, count)],
                    row_ssem.at[level, index],
                    row_rsem.at[level, index],
                    {"rows": me + offset},
                ),
            )

    def finish_level(level):
        for index, (at, offset, first, into, count) in enumerate(row_copies(level)):
            cond = (me - offset >= 0) & (me - offset < rows)
            arrive(
                cond, row_recv.at[level, at, pl.ds(into, count)], row_rsem.at[level, index], row_ssem.at[level, index]
            )
        value = sums[level, 1].reshape(strip, cols, width)
        value = value + row_recv[level, 0].astype(F32) + row_recv[level, 1].astype(F32)
        merge(level + 1, value)

    for turn, level in enumerate(order):
        gather_level(level)
        compute_level(level)
        if turn >= 1:
            finish_level(order[turn - 1])
        if turn >= 2:
            project(order[turn - 2] + 1, False)

    for step in range(1, lines):
        for sign in (1, -1):
            there = mine_z + sign * step
            cond = (there >= 0) & (there < lines)
            arrive(cond, pool_line.at[there], pool_rsem.at[3 + there], pool_ssem.at[0])
    pooled = pool_line[0]
    for line in range(1, lines):
        pooled = pooled + pool_line[line]
    pooled = pooled * (1.0 / (rows * pixels))
    pooled = jax.nn.relu(pooled + branch_bias_ref[4:5, :]).astype(BF16)
    constant = jnp.dot(pooled, proj_ref[4 * width :, :], preferred_element_type=F32)
    constant = constant[0:1, :] + proj_bias_ref[...]

    finish_level(order[-1])
    for level in order[-2:]:
        project(level + 1, False)

    value = jax.nn.relu(total[...] + constant).astype(BF16).reshape(strip, window, width)
    context[...] = value
    out_ref[1 : strip + 1] = value
    for at, (row, offset) in enumerate(((0, -1), (strip - 1, 1))):
        cond = (me + offset >= 0) & (me + offset < rows)
        send(
            cond,
            remote(context.at[row], halo.at[at], halo_ssem.at[at], halo_rsem.at[at], {"rows": me + offset}),
        )
    for at, (row, offset) in enumerate(((0, -1), (strip - 1, 1))):
        place = strip + 1 if at == 0 else 0
        edge = strip - 1 if at == 0 else 0
        cond = (me - offset >= 0) & (me - offset < rows)
        arrive(cond, halo.at[at], halo_rsem.at[at], halo_ssem.at[at])

        @pl.when(cond)
        def _():
            out_ref[place] = halo[at]

        @pl.when(jnp.logical_not(cond))
        def _():
            out_ref[place] = context[edge]

    for cond, copy in pending:
        if cond is None:
            copy.wait_send()
        else:
            pl.when(cond)(copy.wait_send)


def pyramid(features, w_one, w_rate, w_pool, b_branch, w_proj, b_proj):
    strip, cols, depth = features.shape
    levels, taps, shard = w_rate.shape[0], w_rate.shape[1], w_rate.shape[3]
    width = w_one.shape[1]
    rows = lax.axis_size("rows")
    lines = rows // 4
    window = cols // 2 + 16
    pixels = strip * cols
    own = jnp.swapaxes(w_rate, 2, 3)
    sends = levels * (4 + 2 * 3 * (lines - 1) + 2 * lines)
    dma = pltpu.SemaphoreType.DMA
    vmem = pl.BlockSpec(memory_space=pltpu.VMEM)
    return pl.pallas_call(
        lambda *refs: pyramid_kernel((rows, lines, window, None), *refs),
        out_shape=jax.ShapeDtypeStruct((strip + 2, window, width), BF16),
        in_specs=[vmem] * 7,
        out_specs=vmem,
        scratch_shapes=[
            pltpu.VMEM((rows, levels, taps, shard, depth), BF16),
            pltpu.VMEM((levels, 2, strip, cols, depth), BF16),
            pltpu.VMEM((levels, 3, pixels, width), F32),
            pltpu.VMEM((levels, 2, strip, cols, width), BF16),
            pltpu.VMEM((levels, 2, strip, cols, width), BF16),
            pltpu.VMEM((levels + 1, strip, cols, width), BF16),
            pltpu.VMEM((levels + 1, strip, window, width), BF16),
            pltpu.VMEM((strip * window, width), F32),
            pltpu.VMEM((strip, window, width), BF16),
            pltpu.VMEM((2, window, width), BF16),
            pltpu.VMEM((4, 8, width), F32),
            pltpu.VMEM((3, 8, width), F32),
            pltpu.VMEM((lines, 8, width), F32),
            dma((sends,)),
            dma((levels, rows)),
            dma((levels, 4)),
            dma((levels, 4)),
            dma((levels + 1,)),
            dma((levels + 1,)),
            dma((2,)),
            dma((2,)),
            dma((3 + 2 * lines,)),
            dma((3 + lines,)),
        ],
        compiler_params=pltpu.CompilerParams(
            collective_id=0, has_side_effects=True, vmem_limit_bytes=56 * 1024 * 1024
        ),
        cost_estimate=pl.CostEstimate(
            flops=2 * pixels * depth * width * (levels * taps + 1),
            bytes_accessed=2 * levels * taps * depth * width,
            transcendentals=0,
        ),
    )(features, own, w_one, w_pool, b_branch, w_proj, b_proj[None, :])


def context_by_kernel(features, w_one, w_rate, w_pool, b_branch, w_proj, b_proj):
    cols = features.shape[1]
    chan_index = lax.axis_index("chan")
    padded = pyramid(features, w_one, w_rate, w_pool, b_branch, w_proj, b_proj)
    half = cols // 2
    context = jnp.where(chan_index == 0, padded[1:-1, :half], padded[1:-1, 16:])
    coarse = jnp.where(
        chan_index == 0,
        jnp.concatenate([padded[:, :1], padded[:, : half + 1]], axis=1),
        jnp.concatenate([padded[:, 15:], padded[:, -1:]], axis=1),
    )
    return context, coarse


def context_by_collectives(features, w_one, w_rate, w_pool, b_branch, w_proj, b_proj):
    strip_rows, map_cols, group_in = features.shape
    branch_width = w_one.shape[1]
    pixel_count = strip_rows * map_cols
    rows_index = lax.axis_index("rows")
    rows_count = lax.axis_size("rows")
    chan_index = lax.axis_index("chan")
    chan_count = lax.axis_size("chan")
    local_sum = jnp.sum(features, axis=(0, 1), dtype=jnp.float32)
    map_total = strip_rows * rows_count * map_cols
    pool_weight = w_pool.astype(jnp.float32)
    pooled = lax.psum(local_sum, "rows") / map_total
    local_term = jnp.dot(pooled, pool_weight, precision=lax.Precision.HIGHEST)
    pool_pre = lax.psum(local_term, "chan")
    pool_branch = jax.nn.relu(pool_pre + b_branch[4]).astype(jnp.bfloat16)
    head_weight = w_proj[: 4 * branch_width]
    pool_term = jnp.dot(
        pool_branch[None, :], w_proj[4 * branch_width :], preferred_element_type=jnp.float32
    )[0]
    rate_all = lax.all_gather(w_rate, "rows", axis=3, tiled=True)
    rate_outputs = []
    for rate_level in range(3):
        matrix = rate_matrix(features, RATE * (rate_level + 1))
        weight_flat = rate_all[rate_level].reshape(-1, rate_all.shape[3])
        rate_outputs.append(jnp.dot(matrix, weight_flat, preferred_element_type=jnp.float32))
    one_out = jnp.dot(
        features.reshape(pixel_count, group_in), w_one, preferred_element_type=jnp.float32
    )
    partial_value = jnp.concatenate([one_out] + rate_outputs, axis=1).reshape(
        strip_rows, map_cols, 4 * branch_width
    )
    conv_bias = b_branch[:4].reshape(-1)
    summed = lax.psum_scatter(
        partial_value.astype(jnp.bfloat16), "chan", scatter_dimension=2, tiled=True
    ).astype(jnp.float32)
    share_width = summed.shape[2]
    bias_share = lax.dynamic_slice_in_dim(conv_bias, chan_index * share_width, share_width)
    branches = jax.nn.relu(summed + bias_share).astype(jnp.bfloat16)
    weight_share = lax.dynamic_slice_in_dim(head_weight, chan_index * share_width, share_width, 0)
    partial_terms = jnp.dot(
        branches.reshape(-1, share_width), weight_share, preferred_element_type=jnp.float32
    )
    partial_terms = partial_terms.reshape(strip_rows, map_cols, branch_width)
    projected = lax.psum_scatter(
        partial_terms.astype(jnp.bfloat16), "chan", scatter_dimension=1, tiled=True
    ).astype(jnp.float32)
    context = jax.nn.relu(projected + pool_term + b_proj).astype(jnp.bfloat16)
    coarse = padded_2(context, (("rows", 0), ("chan", 1)), 1)
    coarse = edge_copy(coarse, rows_index, rows_count, chan_index, chan_count)
    return context, coarse


def on_device(
    features,
    low_features,
    w_one,
    w_rate,
    w_pool,
    b_branch,
    w_proj,
    b_proj,
    w_low,
    b_low,
    w_dec_up,
    w_dec_low,
    b_dec,
):
    rows_index = lax.axis_index("rows")
    rows_count = lax.axis_size("rows")
    chan_index = lax.axis_index("chan")
    chan_count = lax.axis_size("chan")
    fits = (
        chan_count == 2
        and rows_count % 4 == 0
        and w_rate.shape[3] % 16 == 0
        and features.shape[1] % 32 == 0
        and features.shape[2] % 128 == 0
    )
    make_context = context_by_kernel if fits else context_by_collectives
    context, coarse = make_context(features, w_one, w_rate, w_pool, b_branch, w_proj, b_proj)
    tile_rows_count = context.shape[0]
    tile_cols_count = context.shape[1]
    fine_rows, fine_cols = (low_features.shape[0], low_features.shape[1])
    low_flat = low_features.reshape(fine_rows * fine_cols, low_features.shape[2])
    low_mapped = jax.nn.relu(
        jnp.dot(low_flat, w_low, preferred_element_type=jnp.float32) + b_low
    ).astype(jnp.bfloat16)
    low_mapped = low_mapped.reshape(fine_rows, fine_cols, -1)
    coarse = coarse.astype(jnp.float32)
    upsampled = blend_axis(coarse, 0)[1 : 4 * tile_rows_count + 3]
    upsampled = blend_axis(upsampled, 1)[:, 1 : 4 * tile_cols_count + 3]
    ext_rows, ext_cols = (upsampled.shape[0], upsampled.shape[1])
    row_pos = lax.broadcasted_iota(jnp.int32, (ext_rows, 1, 1), 0)
    col_pos = lax.broadcasted_iota(jnp.int32, (1, ext_cols, 1), 1)
    inside = ((row_pos > 0) | (rows_index > 0)) & (
        (row_pos < ext_rows - 1) | (rows_index < rows_count - 1)
    )
    inside = (
        inside
        & ((col_pos > 0) | (chan_index > 0))
        & ((col_pos < ext_cols - 1) | (chan_index < chan_count - 1))
    )
    up_pad = jnp.where(inside, upsampled, 0.0).astype(jnp.bfloat16)
    low_pad = padded_2(low_mapped, (("rows", 0), ("chan", 1)), 1)
    up_taps = tap_matrix(up_pad, fine_rows, fine_cols)
    low_taps = tap_matrix(low_pad, fine_rows, fine_cols)
    mixed = jnp.dot(
        up_taps, w_dec_up.reshape(-1, w_dec_up.shape[2]), preferred_element_type=jnp.float32
    )
    mixed = mixed + jnp.dot(
        low_taps, w_dec_low.reshape(-1, w_dec_low.shape[2]), preferred_element_type=jnp.float32
    )
    decoded = jax.nn.relu(mixed + b_dec).astype(jnp.bfloat16).reshape(fine_rows, fine_cols, -1)
    return (context, decoded)


def solution(mesh):
    in_specs = (
        P("rows", None, "chan"),
        P("rows", "chan", None),
        P("chan", None),
        P(None, None, "chan", "rows"),
        P("chan", None),
        P(),
        P(),
        P(),
        P(),
        P(),
        P(),
        P(),
        P(),
    )
    out_specs = (P("rows", "chan", None), P("rows", "chan", None))
    return jax.shard_map(
        on_device, mesh=mesh, in_specs=in_specs, out_specs=out_specs, check_vma=False
    )
```

```python
import jax
import jax.numpy as jnp
from jax import lax
from jax.experimental import pallas as pl
from jax.experimental.pallas import tpu as pltpu
from jax.sharding import PartitionSpec as P

RATE = 6


BLEND = (0.875, 0.625, 0.375, 0.125)


def passed_along(block, axis, distance):
    devices = range(lax.axis_size(axis))
    route = [(i - distance, i) for i in devices if i - distance in devices]
    return lax.ppermute(block, axis, route)


def padded_2(array, sides, width):
    for axis, dim in sides:
        devices, length = (lax.axis_size(axis), array.shape[dim])
        up = [(i, (i + 1) % devices) for i in range(devices - 1)]
        down = [(j, i) for i, j in up]
        last = lax.slice_in_dim(array, length - width, length, axis=dim)
        first = lax.slice_in_dim(array, 0, width, axis=dim)
        before = lax.ppermute(last, axis, up)
        after = lax.ppermute(first, axis, down)
        array = jnp.concatenate([before, array, after], axis=dim)
    return array


def move_cols(field, across):
    extent = field.shape[1]
    amount = abs(across)
    padded = jnp.pad(field, ((0, 0), (amount, amount), (0, 0)))
    return padded[:, amount + across : amount + across + extent]


def fetch_rows(features, offset):
    hop_count, remain = divmod(offset, features.shape[0])
    upper_part = features[remain:]
    upper_part = passed_along(upper_part, "rows", -hop_count)
    if remain == 0:
        return upper_part
    lower_part = features[:remain]
    lower_part = passed_along(lower_part, "rows", -hop_count - 1)
    return jnp.concatenate([upper_part, lower_part], axis=0)


def rate_matrix(features, spacing):
    sources = (fetch_rows(features, -spacing), features, fetch_rows(features, spacing))
    pieces = [
        move_cols(source, (col_step - 1) * spacing) for source in sources for col_step in range(3)
    ]
    stacked = jnp.concatenate(pieces, axis=2)
    return stacked.reshape(-1, stacked.shape[2])


def blend_axis(field, axis_pos):
    count_in = field.shape[axis_pos]
    lower_half = lax.slice_in_dim(field, 0, count_in - 1, axis=axis_pos)
    upper_half = lax.slice_in_dim(field, 1, count_in, axis=axis_pos)
    blended = jnp.stack(
        [factor * lower_half + (1.0 - factor) * upper_half for factor in BLEND], axis=axis_pos + 1
    )
    target = list(lower_half.shape)
    target[axis_pos] = 4 * (count_in - 1)
    return blended.reshape(target)


def edge_copy(padded, rows_index, rows_count, chan_index, chan_count):
    top_row = jnp.where(rows_index == 0, padded[1:2], padded[0:1])
    bottom_row = jnp.where(rows_index == rows_count - 1, padded[-2:-1], padded[-1:])
    padded = jnp.concatenate([top_row, padded[1:-1], bottom_row], axis=0)
    left_col = jnp.where(chan_index == 0, padded[:, 1:2], padded[:, 0:1])
    right_col = jnp.where(chan_index == chan_count - 1, padded[:, -2:-1], padded[:, -1:])
    return jnp.concatenate([left_col, padded[:, 1:-1], right_col], axis=1)


def tap_matrix(padded, out_rows, out_cols):
    pieces = [
        padded[row_step : row_step + out_rows, col_step : col_step + out_cols]
        for row_step in range(3)
        for col_step in range(3)
    ]
    stacked = jnp.concatenate(pieces, axis=2)
    return stacked.reshape(out_rows * out_cols, -1)


F32 = jnp.float32
BF16 = jnp.bfloat16
MESH = pl.DeviceIdType.MESH


def dot_t(lhs, rhs):
    return lax.dot_general(lhs, rhs, (((1,), (1,)), ((), ())), preferred_element_type=F32)


def pyramid_kernel(
    geometry,
    f_ref, own_ref, one_ref, pool_ref, branch_bias_ref, proj_ref, proj_bias_ref,
    low_ref, low_weight_ref, low_bias_ref,
    out_ref, low_out_ref,
    wbuf, shifted, sums, row_send, row_recv, merged, chan_recv, total, context, halo,
    pool_send, pool_recv, pool_line,
    gather_send, gather_recv, row_ssem, row_rsem, chan_ssem, chan_rsem, halo_ssem, halo_rsem,
    pool_ssem, pool_rsem,
    low_edge, low_send, low_recv, low_rows_send, low_rows_recv, low_ssem, low_rsem,
):
    rows, lines, window, low_width = geometry
    fine_rows, fine_cols, low_depth = low_ref.shape
    packed = low_weight_ref.shape[1]
    strip, cols, depth = f_ref.shape
    width = one_ref.shape[1]
    pixels = strip * cols
    me = lax.axis_index("rows")
    chan = lax.axis_index("chan")
    mine_z = me // 4
    mine_y = (me // 2) % 2
    core_peer = me + 1 - 2 * (me % 2)
    y_peer = me + 2 - 4 * mine_y
    chan_peer = 1 - chan
    levels = own_ref.shape[0]
    pending = []

    def remote(src, dst, ssem, rsem, device):
        return pltpu.make_async_remote_copy(
            src_ref=src, dst_ref=dst, send_sem=ssem, recv_sem=rsem, device_id=device, device_id_type=MESH
        )

    def send(cond, copy):
        if cond is None:
            copy.start()
        else:
            pl.when(cond)(copy.start)
        pending.append((cond, copy))

    def arrive(cond, ref, rsem, ssem):
        copy = remote(ref, ref, ssem, rsem, {"chan": chan_peer})
        if cond is None:
            copy.wait_recv()
        else:
            pl.when(cond)(copy.wait_recv)

    row_recv[...] = jnp.zeros_like(row_recv)
    low_rows_recv[...] = jnp.zeros_like(low_rows_recv)
    wbuf[me] = own_ref[...]

    barrier = pltpu.get_barrier_semaphore()
    for step in range(1, rows):
        pl.semaphore_signal(
            barrier, inc=1, device_id={"rows": lax.rem(me + step, rows)}, device_id_type=MESH
        )
    pl.semaphore_signal(barrier, inc=1, device_id={"chan": chan_peer}, device_id_type=MESH)
    pl.semaphore_wait(barrier, rows)

    counter = [0]

    def pass_shard(cond, source, level, target):
        index = counter[0]
        counter[0] += 1
        slot = wbuf.at[source, level]
        send(
            cond,
            remote(slot, slot, gather_send.at[index], gather_recv.at[level, source], {"rows": target}),
        )

    def shard_here(cond, source, level):
        arrive(cond, wbuf.at[source, level], gather_recv.at[level, source], gather_send.at[0])

    def both(one, other):
        return other if one is None else one & other

    order = list(range(levels))[::-1]
    for level in order:
        pass_shard(mine_z + 1 < lines, me, level, me + 4)
        pass_shard(mine_z > 0, me, level, me - 4)
        pass_shard(None, me, level, y_peer)
        pass_shard(None, me, level, core_peer)

    def flat():
        return f_ref[...].reshape(pixels, depth)

    local = jnp.zeros((8, depth), F32)
    for row in range(strip):
        block = f_ref[row].astype(F32).reshape(cols // 8, 8, depth)
        local = local + jnp.sum(block, axis=0)
    local = jnp.broadcast_to(jnp.sum(local, axis=0, keepdims=True), (8, depth))
    pool_send[0] = jnp.dot(
        local, pool_ref[...].astype(F32), precision=lax.Precision.HIGHEST, preferred_element_type=F32
    )
    peers = ({"chan": chan_peer}, {"rows": core_peer}, {"rows": y_peer})

    def pool_round(turn):
        send(
            None,
            remote(
                pool_send.at[turn], pool_recv.at[turn], pool_ssem.at[turn], pool_rsem.at[turn], peers[turn]
            ),
        )

    def pool_add(turn):
        arrive(None, pool_recv.at[turn], pool_rsem.at[turn], pool_ssem.at[turn])
        pool_send[turn + 1] = pool_send[turn] + pool_recv[turn]

    def merge(slot, value):
        merged[slot] = value.astype(BF16).reshape(strip, cols, width)
        start = pl.multiple_of(chan_peer * (cols - window), 16)
        send(
            None,
            remote(
                merged.at[slot, :, pl.ds(start, window), :],
                chan_recv.at[slot],
                chan_ssem.at[slot],
                chan_rsem.at[slot],
                {"chan": chan_peer},
            ),
        )

    def project(slot, first):
        arrive(None, chan_recv.at[slot], chan_rsem.at[slot], chan_ssem.at[slot])
        start = pl.multiple_of(chan * (cols - window), 16)
        value = merged[slot, :, pl.ds(start, window), :].astype(F32) + chan_recv[slot].astype(F32)
        value = jax.nn.relu(value + branch_bias_ref[slot : slot + 1, :].reshape(1, 1, width))
        value = value.astype(BF16).reshape(strip * window, width)
        term = jnp.dot(
            value, proj_ref[slot * width : (slot + 1) * width, :], preferred_element_type=F32
        )
        if first:
            total[...] = term
        else:
            total[...] += term

    def shift_level(level):
        spacing = RATE * (level + 1)
        pos = lax.broadcasted_iota(jnp.int32, (cols, depth), 0)
        for row in range(strip):
            value = f_ref[row].astype(F32)
            before = jnp.where(pos < spacing, 0.0, pltpu.roll(value, spacing, 0))
            after = jnp.where(pos >= cols - spacing, 0.0, pltpu.roll(value, cols - spacing, 0))
            shifted[level, 0, row] = before.astype(BF16)
            shifted[level, 1, row] = after.astype(BF16)

    def mapped_low(value):
        return jax.nn.relu(
            jnp.dot(value, low_weight_ref[...], preferred_element_type=F32) + low_bias_ref[...]
        )

    @pl.loop(0, fine_rows)
    def _(row):
        first = low_ref[row, 0:16, :].astype(F32)
        last = low_ref[row, fine_cols - 16 : fine_cols, :].astype(F32)
        low_edge[pl.ds(row, 1), :] = jnp.where(chan == 0, last[15:16], first[0:1])

    low_send[...] = mapped_low(low_edge[...].astype(BF16))
    send(
        None,
        remote(low_send, low_recv, low_ssem.at[0], low_rsem.at[0], {"chan": chan_peer}),
    )

    pool_round(0)
    merge(0, jnp.dot(flat(), one_ref[...], preferred_element_type=F32))
    pool_add(0)
    pool_round(1)
    shift_level(order[0])
    pool_add(1)
    pool_round(2)

    arrive(None, low_recv, low_rsem.at[0], low_ssem.at[0])

    @pl.loop(0, fine_rows)
    def _(row):
        value = mapped_low(low_ref[row])
        pos = lax.broadcasted_iota(jnp.int32, (fine_cols, packed), 0)
        lane = lax.broadcasted_iota(jnp.int32, (fine_cols, packed), 1)
        outer = low_recv[pl.ds(row, 1), :]
        left = jnp.where(chan == 0, 0.0, outer)
        right = jnp.where(chan == 0, outer, 0.0)
        before = jnp.where(pos == 0, left, pltpu.roll(value, 1, 0))
        after = jnp.where(pos == fine_cols - 1, right, pltpu.roll(value, fine_cols - 1, 0))
        value = jnp.where(lane < low_width, before, jnp.where(lane < 2 * low_width, value, after))
        low_out_ref[row + 1] = value.astype(BF16)

    low_rows_send[0] = low_out_ref[1]
    low_rows_send[1] = low_out_ref[fine_rows]
    for at, offset in enumerate((-1, 1)):
        send(
            (me + offset >= 0) & (me + offset < rows),
            remote(
                low_rows_send.at[at],
                low_rows_recv.at[at],
                low_ssem.at[1 + at],
                low_rsem.at[1 + at],
                {"rows": me + offset},
            ),
        )
    for level in order[1:]:
        shift_level(level)
    pool_add(2)
    pool_line[mine_z] = pool_send[3]
    for step in range(1, lines):
        for at, sign in enumerate((1, -1)):
            there = mine_z + sign * step
            cond = (there >= 0) & (there < lines)
            send(
                cond,
                remote(
                    pool_send.at[3],
                    pool_line.at[mine_z],
                    pool_ssem.at[3 + 2 * (step - 1) + at],
                    pool_rsem.at[3 + mine_z],
                    {"rows": me + 4 * sign * step},
                ),
            )
    project(0, True)

    def gather_level(level):
        for step in range(1, lines):
            for sign in (-1, 1):
                source = me + 4 * sign * step
                here = (mine_z + sign * step >= 0) & (mine_z + sign * step < lines)
                beyond = here & (mine_z - sign >= 0) & (mine_z - sign < lines)
                shard_here(here, source, level)
                pass_shard(beyond, source, level, me - 4 * sign)
                pass_shard(here, source, level, y_peer)
                pass_shard(here, source, level, core_peer)
        for step in range(lines):
            for sign in (-1, 1) if step else (1,):
                source = y_peer + 4 * sign * step
                here = (mine_z + sign * step >= 0) & (mine_z + sign * step < lines)
                shard_here(here, source, level)
                pass_shard(here, source, level, core_peer)
        for line in range(lines):
            for y in range(2):
                shard_here(None, line * 4 + y * 2 + 1 - me % 2, level)

    def row_copies(level):
        hop, remain = divmod(RATE * (level + 1), strip)
        found = []
        if remain < strip:
            found.append((0, hop, 0, remain, strip - remain))
            found.append((1, -hop, remain, 0, strip - remain))
        if remain > 0:
            found.append((0, hop + 1, strip - remain, 0, remain))
            found.append((1, -hop - 1, 0, strip - remain, remain))
        return found

    def compute_level(level):
        spread = levels * 3

        @pl.loop(0, 3)
        def _(down):
            value = None
            for across in range(3):
                weight = wbuf[:, level, 3 * down + across].reshape(width, depth)
                side = f_ref[...] if across == 1 else shifted[level, across // 2]
                term = dot_t(side.reshape(pixels, depth), weight)
                value = term if value is None else value + term
            sums[level, down] = value

        for at, down in enumerate((0, 2)):
            row_send[level, at] = sums[level, down].astype(BF16).reshape(strip, cols, width)
        for index, (at, offset, first, into, count) in enumerate(row_copies(level)):
            cond = (me + offset >= 0) & (me + offset < rows)
            send(
                cond,
                remote(
                    row_send.at[level, at, pl.ds(first, count)],
                    row_recv.at[level, at, pl.ds(into, count)],
                    row_ssem.at[level, index],
                    row_rsem.at[level, index],
                    {"rows": me + offset},
                ),
            )

    def finish_level(level):
        for index, (at, offset, first, into, count) in enumerate(row_copies(level)):
            cond = (me - offset >= 0) & (me - offset < rows)
            arrive(
                cond, row_recv.at[level, at, pl.ds(into, count)], row_rsem.at[level, index], row_ssem.at[level, index]
            )
        value = sums[level, 1].reshape(strip, cols, width)
        value = value + row_recv[level, 0].astype(F32) + row_recv[level, 1].astype(F32)
        merge(level + 1, value)

    for turn, level in enumerate(order):
        gather_level(level)
        compute_level(level)
        if turn >= 1:
            finish_level(order[turn - 1])
        if turn >= 2:
            project(order[turn - 2] + 1, False)

    for at, (offset, place) in enumerate(((-1, fine_rows + 1), (1, 0))):
        cond = (me - offset >= 0) & (me - offset < rows)
        arrive(cond, low_rows_recv.at[at], low_rsem.at[1 + at], low_ssem.at[1 + at])
        low_out_ref[place] = low_rows_recv[at]

    for step in range(1, lines):
        for sign in (1, -1):
            there = mine_z + sign * step
            cond = (there >= 0) & (there < lines)
            arrive(cond, pool_line.at[there], pool_rsem.at[3 + there], pool_ssem.at[0])
    pooled = pool_line[0]
    for line in range(1, lines):
        pooled = pooled + pool_line[line]
    pooled = pooled * (1.0 / (rows * pixels))
    pooled = jax.nn.relu(pooled + branch_bias_ref[4:5, :]).astype(BF16)
    constant = jnp.dot(pooled, proj_ref[4 * width :, :], preferred_element_type=F32)
    constant = constant[0:1, :] + proj_bias_ref[...]

    finish_level(order[-1])
    for level in order[-2:]:
        project(level + 1, False)

    value = jax.nn.relu(total[...] + constant).astype(BF16).reshape(strip, window, width)
    context[...] = value
    out_ref[1 : strip + 1] = value
    for at, (row, offset) in enumerate(((0, -1), (strip - 1, 1))):
        cond = (me + offset >= 0) & (me + offset < rows)
        send(
            cond,
            remote(context.at[row], halo.at[at], halo_ssem.at[at], halo_rsem.at[at], {"rows": me + offset}),
        )
    for at, (row, offset) in enumerate(((0, -1), (strip - 1, 1))):
        place = strip + 1 if at == 0 else 0
        edge = strip - 1 if at == 0 else 0
        cond = (me - offset >= 0) & (me - offset < rows)
        arrive(cond, halo.at[at], halo_rsem.at[at], halo_ssem.at[at])

        @pl.when(cond)
        def _():
            out_ref[place] = halo[at]

        @pl.when(jnp.logical_not(cond))
        def _():
            out_ref[place] = context[edge]

    for cond, copy in pending:
        if cond is None:
            copy.wait_send()
        else:
            pl.when(cond)(copy.wait_send)


def pyramid(features, w_one, w_rate, w_pool, b_branch, w_proj, b_proj, low_features, w_low, b_low):
    strip, cols, depth = features.shape
    levels, taps, shard = w_rate.shape[0], w_rate.shape[1], w_rate.shape[3]
    width = w_one.shape[1]
    rows = lax.axis_size("rows")
    lines = rows // 4
    window = cols // 2 + 16
    pixels = strip * cols
    own = jnp.swapaxes(w_rate, 2, 3)
    sends = levels * (4 + 2 * 3 * (lines - 1) + 2 * lines)
    fine_rows, fine_cols, low_depth = low_features.shape
    low_width = w_low.shape[1]
    packed = pl.cdiv(3 * low_width, 128) * 128
    rest = packed - 3 * low_width
    low_weight = jnp.pad(jnp.concatenate([w_low] * 3, axis=1), ((0, 0), (0, rest)))
    low_bias = jnp.pad(jnp.concatenate([b_low] * 3), (0, rest))[None, :]
    dma = pltpu.SemaphoreType.DMA
    vmem = pl.BlockSpec(memory_space=pltpu.VMEM)
    return pl.pallas_call(
        lambda *refs: pyramid_kernel((rows, lines, window, low_width), *refs),
        out_shape=(
            jax.ShapeDtypeStruct((strip + 2, window, width), BF16),
            jax.ShapeDtypeStruct((fine_rows + 2, fine_cols, packed), BF16),
        ),
        in_specs=[vmem] * 10,
        out_specs=(vmem, vmem),
        scratch_shapes=[
            pltpu.VMEM((rows, levels, taps, shard, depth), BF16),
            pltpu.VMEM((levels, 2, strip, cols, depth), BF16),
            pltpu.VMEM((levels, 3, pixels, width), F32),
            pltpu.VMEM((levels, 2, strip, cols, width), BF16),
            pltpu.VMEM((levels, 2, strip, cols, width), BF16),
            pltpu.VMEM((levels + 1, strip, cols, width), BF16),
            pltpu.VMEM((levels + 1, strip, window, width), BF16),
            pltpu.VMEM((strip * window, width), F32),
            pltpu.VMEM((strip, window, width), BF16),
            pltpu.VMEM((2, window, width), BF16),
            pltpu.VMEM((4, 8, width), F32),
            pltpu.VMEM((3, 8, width), F32),
            pltpu.VMEM((lines, 8, width), F32),
            dma((sends,)),
            dma((levels, rows)),
            dma((levels, 4)),
            dma((levels, 4)),
            dma((levels + 1,)),
            dma((levels + 1,)),
            dma((2,)),
            dma((2,)),
            dma((3 + 2 * lines,)),
            dma((3 + lines,)),
            pltpu.VMEM((fine_rows, low_depth), F32),
            pltpu.VMEM((fine_rows, packed), F32),
            pltpu.VMEM((fine_rows, packed), F32),
            pltpu.VMEM((2, fine_cols, packed), BF16),
            pltpu.VMEM((2, fine_cols, packed), BF16),
            dma((3,)),
            dma((3,)),
        ],
        compiler_params=pltpu.CompilerParams(
            collective_id=0, has_side_effects=True, vmem_limit_bytes=56 * 1024 * 1024
        ),
        cost_estimate=pl.CostEstimate(
            flops=2 * pixels * depth * width * (levels * taps + 1),
            bytes_accessed=2 * levels * taps * depth * width,
            transcendentals=0,
        ),
    )(
        features, own, w_one, w_pool, b_branch, w_proj, b_proj[None, :],
        low_features, low_weight, low_bias,
    )


def decoder_kernel(
    strip, coarse_ref, low_ref, blend_ref, up_weight_ref, low_weight_ref, bias_ref, out_ref, fine
):
    at = pl.program_id(0)
    me = lax.axis_index("rows")
    rows = lax.axis_size("rows")
    block, fine_cols, width = out_ref.shape
    fine_rows = fine.shape[0] - 2
    window, depth = coarse_ref.shape[1], coarse_ref.shape[2]

    @pl.when(at == 0)
    def _():
        for row in range(fine_rows + 2):
            pair, phase = divmod(row + 1, 4)
            source = coarse_ref[pair : pair + 2].reshape(2 * window, depth)
            for across in range(3):
                value = jnp.dot(
                    blend_ref[phase, across * fine_cols : (across + 1) * fine_cols, :],
                    source,
                    preferred_element_type=F32,
                )
                if row == 0:
                    value = jnp.where(me == 0, 0.0, value)
                if row == fine_rows + 1:
                    value = jnp.where(me == rows - 1, 0.0, value)
                fine[row, :, across * depth : (across + 1) * depth] = value.astype(BF16)

    total = None
    for down in range(3):
        up = fine[pl.ds(at * block + down, block)].reshape(block * fine_cols, 3 * depth)
        low = low_ref[pl.ds(at * block + down, block)].reshape(block * fine_cols, low_ref.shape[2])
        term = jnp.dot(up, up_weight_ref[down], preferred_element_type=F32)
        term = term + jnp.dot(low, low_weight_ref[down], preferred_element_type=F32)
        total = term if total is None else total + term
    total = jax.nn.relu(total + bias_ref[...])
    out_ref[...] = total.astype(BF16).reshape(block, fine_cols, width)


def blend_matrices(half, window, chan_index):
    fine_cols = 4 * half
    shape = (4, 3, fine_cols, 2, window)
    phase, across, pos, lower, col = (lax.broadcasted_iota(jnp.int32, shape, d) for d in range(5))
    place = pos + across - 1
    pair, col_phase = (place + 2) // 4, (place + 2) % 4
    first = jnp.clip(chan_index * half + pair - 1, 0, 2 * half - 1) - chan_index * (2 * half - window)
    second = jnp.clip(chan_index * half + pair, 0, 2 * half - 1) - chan_index * (2 * half - window)
    col_upper = 0.875 - 0.25 * col_phase.astype(F32)
    factor = jnp.where(col == first, col_upper, 0.0) + jnp.where(col == second, 1.0 - col_upper, 0.0)
    row_upper = 0.875 - 0.25 * phase.astype(F32)
    factor = factor * jnp.where(lower == 0, row_upper, 1.0 - row_upper)
    whole = chan_index * fine_cols + place
    factor = jnp.where((whole >= 0) & (whole < 2 * fine_cols), factor, 0.0)
    return factor.astype(BF16).reshape(4, 3 * fine_cols, 2 * window)


def whole_by_kernels(
    features, low_features, w_one, w_rate, w_pool, b_branch, w_proj, b_proj, w_low, b_low,
    w_dec_up, w_dec_low, b_dec,
):
    strip, cols = features.shape[0], features.shape[1]
    fine_rows, fine_cols = low_features.shape[0], low_features.shape[1]
    depth, width = w_dec_up.shape[1], w_dec_up.shape[2]
    chan_index = lax.axis_index("chan")
    half = cols // 2
    padded, low_packed = pyramid(
        features, w_one, w_rate, w_pool, b_branch, w_proj, b_proj, low_features, w_low, b_low
    )
    window, packed = padded.shape[1], low_packed.shape[2]
    context = jnp.where(chan_index == 0, padded[1:-1, :half], padded[1:-1, window - half :])
    up_weight = w_dec_up.reshape(3, 3 * depth, width)
    low_weight = w_dec_low.reshape(3, -1, width)
    low_weight = jnp.pad(low_weight, ((0, 0), (0, packed - low_weight.shape[1]), (0, 0)))
    blend = blend_matrices(half, window, chan_index)
    whole = pl.BlockSpec(memory_space=pltpu.VMEM)
    block = 4
    pixels = fine_rows * fine_cols
    decoded = pl.pallas_call(
        lambda *refs: decoder_kernel(strip, *refs),
        out_shape=jax.ShapeDtypeStruct((fine_rows, fine_cols, width), BF16),
        grid=(fine_rows // block,),
        in_specs=[whole] * 6,
        out_specs=pl.BlockSpec((block, fine_cols, width), lambda i: (i, 0, 0)),
        scratch_shapes=[pltpu.VMEM((fine_rows + 2, fine_cols, 3 * depth), BF16)],
        compiler_params=pltpu.CompilerParams(vmem_limit_bytes=48 * 1024 * 1024),
        cost_estimate=pl.CostEstimate(
            flops=2 * pixels * width * (9 * depth + 3 * packed),
            bytes_accessed=2 * pixels * (width + packed),
            transcendentals=0,
        ),
    )(padded, low_packed, blend, up_weight, low_weight, b_dec[None, :])
    return context, decoded


def context_by_collectives(features, w_one, w_rate, w_pool, b_branch, w_proj, b_proj):
    strip_rows, map_cols, group_in = features.shape
    branch_width = w_one.shape[1]
    pixel_count = strip_rows * map_cols
    rows_index = lax.axis_index("rows")
    rows_count = lax.axis_size("rows")
    chan_index = lax.axis_index("chan")
    chan_count = lax.axis_size("chan")
    local_sum = jnp.sum(features, axis=(0, 1), dtype=jnp.float32)
    map_total = strip_rows * rows_count * map_cols
    pool_weight = w_pool.astype(jnp.float32)
    pooled = lax.psum(local_sum, "rows") / map_total
    local_term = jnp.dot(pooled, pool_weight, precision=lax.Precision.HIGHEST)
    pool_pre = lax.psum(local_term, "chan")
    pool_branch = jax.nn.relu(pool_pre + b_branch[4]).astype(jnp.bfloat16)
    head_weight = w_proj[: 4 * branch_width]
    pool_term = jnp.dot(
        pool_branch[None, :], w_proj[4 * branch_width :], preferred_element_type=jnp.float32
    )[0]
    rate_all = lax.all_gather(w_rate, "rows", axis=3, tiled=True)
    rate_outputs = []
    for rate_level in range(3):
        matrix = rate_matrix(features, RATE * (rate_level + 1))
        weight_flat = rate_all[rate_level].reshape(-1, rate_all.shape[3])
        rate_outputs.append(jnp.dot(matrix, weight_flat, preferred_element_type=jnp.float32))
    one_out = jnp.dot(
        features.reshape(pixel_count, group_in), w_one, preferred_element_type=jnp.float32
    )
    partial_value = jnp.concatenate([one_out] + rate_outputs, axis=1).reshape(
        strip_rows, map_cols, 4 * branch_width
    )
    conv_bias = b_branch[:4].reshape(-1)
    summed = lax.psum_scatter(
        partial_value.astype(jnp.bfloat16), "chan", scatter_dimension=2, tiled=True
    ).astype(jnp.float32)
    share_width = summed.shape[2]
    bias_share = lax.dynamic_slice_in_dim(conv_bias, chan_index * share_width, share_width)
    branches = jax.nn.relu(summed + bias_share).astype(jnp.bfloat16)
    weight_share = lax.dynamic_slice_in_dim(head_weight, chan_index * share_width, share_width, 0)
    partial_terms = jnp.dot(
        branches.reshape(-1, share_width), weight_share, preferred_element_type=jnp.float32
    )
    partial_terms = partial_terms.reshape(strip_rows, map_cols, branch_width)
    projected = lax.psum_scatter(
        partial_terms.astype(jnp.bfloat16), "chan", scatter_dimension=1, tiled=True
    ).astype(jnp.float32)
    context = jax.nn.relu(projected + pool_term + b_proj).astype(jnp.bfloat16)
    coarse = padded_2(context, (("rows", 0), ("chan", 1)), 1)
    coarse = edge_copy(coarse, rows_index, rows_count, chan_index, chan_count)
    return context, coarse


def on_device(
    features,
    low_features,
    w_one,
    w_rate,
    w_pool,
    b_branch,
    w_proj,
    b_proj,
    w_low,
    b_low,
    w_dec_up,
    w_dec_low,
    b_dec,
):
    rows_index = lax.axis_index("rows")
    rows_count = lax.axis_size("rows")
    chan_index = lax.axis_index("chan")
    chan_count = lax.axis_size("chan")
    fits = (
        chan_count == 2
        and rows_count % 4 == 0
        and w_rate.shape[3] % 16 == 0
        and features.shape[1] % 32 == 0
        and features.shape[2] % 128 == 0
        and features.shape[0] % 2 == 0
        and low_features.shape[0] == 4 * features.shape[0]
        and low_features.shape[0] % 16 == 0
        and 2 * low_features.shape[1] == 4 * features.shape[1]
    )
    if fits:
        return whole_by_kernels(
            features, low_features, w_one, w_rate, w_pool, b_branch, w_proj, b_proj, w_low, b_low,
            w_dec_up, w_dec_low, b_dec,
        )
    context, coarse = context_by_collectives(
        features, w_one, w_rate, w_pool, b_branch, w_proj, b_proj
    )
    tile_rows_count = context.shape[0]
    tile_cols_count = context.shape[1]
    fine_rows, fine_cols = (low_features.shape[0], low_features.shape[1])
    low_flat = low_features.reshape(fine_rows * fine_cols, low_features.shape[2])
    low_mapped = jax.nn.relu(
        jnp.dot(low_flat, w_low, preferred_element_type=jnp.float32) + b_low
    ).astype(jnp.bfloat16)
    low_mapped = low_mapped.reshape(fine_rows, fine_cols, -1)
    coarse = coarse.astype(jnp.float32)
    upsampled = blend_axis(coarse, 0)[1 : 4 * tile_rows_count + 3]
    upsampled = blend_axis(upsampled, 1)[:, 1 : 4 * tile_cols_count + 3]
    ext_rows, ext_cols = (upsampled.shape[0], upsampled.shape[1])
    row_pos = lax.broadcasted_iota(jnp.int32, (ext_rows, 1, 1), 0)
    col_pos = lax.broadcasted_iota(jnp.int32, (1, ext_cols, 1), 1)
    inside = ((row_pos > 0) | (rows_index > 0)) & (
        (row_pos < ext_rows - 1) | (rows_index < rows_count - 1)
    )
    inside = (
        inside
        & ((col_pos > 0) | (chan_index > 0))
        & ((col_pos < ext_cols - 1) | (chan_index < chan_count - 1))
    )
    up_pad = jnp.where(inside, upsampled, 0.0).astype(jnp.bfloat16)
    low_pad = padded_2(low_mapped, (("rows", 0), ("chan", 1)), 1)
    up_taps = tap_matrix(up_pad, fine_rows, fine_cols)
    low_taps = tap_matrix(low_pad, fine_rows, fine_cols)
    mixed = jnp.dot(
        up_taps, w_dec_up.reshape(-1, w_dec_up.shape[2]), preferred_element_type=jnp.float32
    )
    mixed = mixed + jnp.dot(
        low_taps, w_dec_low.reshape(-1, w_dec_low.shape[2]), preferred_element_type=jnp.float32
    )
    decoded = jax.nn.relu(mixed + b_dec).astype(jnp.bfloat16).reshape(fine_rows, fine_cols, -1)
    return (context, decoded)


def solution(mesh):
    in_specs = (
        P("rows", None, "chan"),
        P("rows", "chan", None),
        P("chan", None),
        P(None, None, "chan", "rows"),
        P("chan", None),
        P(),
        P(),
        P(),
        P(),
        P(),
        P(),
        P(),
        P(),
    )
    out_specs = (P("rows", "chan", None), P("rows", "chan", None))
    return jax.shard_map(
        on_device, mesh=mesh, in_specs=in_specs, out_specs=out_specs, check_vma=False
    )
```

```python
import jax
import jax.numpy as jnp
from jax import lax
from jax.experimental import pallas as pl
from jax.experimental.pallas import tpu as pltpu
from jax.sharding import PartitionSpec as P

RATE = 6


BLEND = (0.875, 0.625, 0.375, 0.125)


def passed_along(block, axis, distance):
    devices = range(lax.axis_size(axis))
    route = [(i - distance, i) for i in devices if i - distance in devices]
    return lax.ppermute(block, axis, route)


def padded_2(array, sides, width):
    for axis, dim in sides:
        devices, length = (lax.axis_size(axis), array.shape[dim])
        up = [(i, (i + 1) % devices) for i in range(devices - 1)]
        down = [(j, i) for i, j in up]
        last = lax.slice_in_dim(array, length - width, length, axis=dim)
        first = lax.slice_in_dim(array, 0, width, axis=dim)
        before = lax.ppermute(last, axis, up)
        after = lax.ppermute(first, axis, down)
        array = jnp.concatenate([before, array, after], axis=dim)
    return array


def move_cols(field, across):
    extent = field.shape[1]
    amount = abs(across)
    padded = jnp.pad(field, ((0, 0), (amount, amount), (0, 0)))
    return padded[:, amount + across : amount + across + extent]


def fetch_rows(features, offset):
    hop_count, remain = divmod(offset, features.shape[0])
    upper_part = features[remain:]
    upper_part = passed_along(upper_part, "rows", -hop_count)
    if remain == 0:
        return upper_part
    lower_part = features[:remain]
    lower_part = passed_along(lower_part, "rows", -hop_count - 1)
    return jnp.concatenate([upper_part, lower_part], axis=0)


def rate_matrix(features, spacing):
    sources = (fetch_rows(features, -spacing), features, fetch_rows(features, spacing))
    pieces = [
        move_cols(source, (col_step - 1) * spacing) for source in sources for col_step in range(3)
    ]
    stacked = jnp.concatenate(pieces, axis=2)
    return stacked.reshape(-1, stacked.shape[2])


def blend_axis(field, axis_pos):
    count_in = field.shape[axis_pos]
    lower_half = lax.slice_in_dim(field, 0, count_in - 1, axis=axis_pos)
    upper_half = lax.slice_in_dim(field, 1, count_in, axis=axis_pos)
    blended = jnp.stack(
        [factor * lower_half + (1.0 - factor) * upper_half for factor in BLEND], axis=axis_pos + 1
    )
    target = list(lower_half.shape)
    target[axis_pos] = 4 * (count_in - 1)
    return blended.reshape(target)


def edge_copy(padded, rows_index, rows_count, chan_index, chan_count):
    top_row = jnp.where(rows_index == 0, padded[1:2], padded[0:1])
    bottom_row = jnp.where(rows_index == rows_count - 1, padded[-2:-1], padded[-1:])
    padded = jnp.concatenate([top_row, padded[1:-1], bottom_row], axis=0)
    left_col = jnp.where(chan_index == 0, padded[:, 1:2], padded[:, 0:1])
    right_col = jnp.where(chan_index == chan_count - 1, padded[:, -2:-1], padded[:, -1:])
    return jnp.concatenate([left_col, padded[:, 1:-1], right_col], axis=1)


def tap_matrix(padded, out_rows, out_cols):
    pieces = [
        padded[row_step : row_step + out_rows, col_step : col_step + out_cols]
        for row_step in range(3)
        for col_step in range(3)
    ]
    stacked = jnp.concatenate(pieces, axis=2)
    return stacked.reshape(out_rows * out_cols, -1)


F32 = jnp.float32
BF16 = jnp.bfloat16
MESH = pl.DeviceIdType.MESH


def dot_t(lhs, rhs):
    return lax.dot_general(lhs, rhs, (((1,), (1,)), ((), ())), preferred_element_type=F32)


def pyramid_kernel(
    geometry,
    f_ref, own_ref, one_ref, pool_ref, branch_bias_ref, proj_ref, proj_bias_ref,
    low_ref, low_weight_ref, low_bias_ref,
    out_ref, low_out_ref,
    wbuf, maps, shifted, row_send, row_recv, merged, chan_recv, total, context, halo,
    pool_send, pool_recv, pool_line,
    own_send, gather_send, gather_recv, row_ssem, row_rsem, chan_ssem, chan_rsem, halo_ssem, halo_rsem,
    pool_ssem, pool_rsem,
    maps_ssem, maps_rsem, low_edge, low_send, low_recv, low_rows_send, low_rows_recv, low_ssem, low_rsem,
):
    rows, lines, window, low_width = geometry
    fine_rows, fine_cols, low_depth = low_ref.shape
    packed = low_weight_ref.shape[1]
    strip, cols, depth = f_ref.shape
    width = one_ref.shape[1]
    pixels = strip * cols
    me = lax.axis_index("rows")
    chan = lax.axis_index("chan")
    mine_z = me // 4
    mine_y = (me // 2) % 2
    mine_c = me % 2
    half = mine_z % 2
    twin = me + 4 - 8 * half
    sources = lines // 2
    own_half = mine_z // sources
    own_slot = me - own_half * (rows // 2)
    part = width // 2
    lanes = pl.ds(pl.multiple_of(half * part, part), part)
    core_peer = me + 1 - 2 * (me % 2)
    y_peer = me + 2 - 4 * mine_y
    chan_peer = 1 - chan
    levels = own_ref.shape[0]
    pending = []

    def remote(src, dst, ssem, rsem, device):
        return pltpu.make_async_remote_copy(
            src_ref=src, dst_ref=dst, send_sem=ssem, recv_sem=rsem, device_id=device, device_id_type=MESH
        )

    def send(cond, copy):
        if cond is None:
            copy.start()
        else:
            pl.when(cond)(copy.start)
        pending.append((cond, copy))

    def arrive(cond, ref, rsem, ssem):
        copy = remote(ref, ref, ssem, rsem, {"chan": chan_peer})
        if cond is None:
            copy.wait_recv()
        else:
            pl.when(cond)(copy.wait_recv)

    row_recv[...] = jnp.zeros_like(row_recv)
    low_rows_recv[...] = jnp.zeros_like(low_rows_recv)
    maps[0] = f_ref[...]

    @pl.when(own_half == half)
    def _():
        wbuf[own_slot] = own_ref[...]


    barrier = pltpu.get_barrier_semaphore()
    for step in range(1, rows):
        pl.semaphore_signal(
            barrier, inc=1, device_id={"rows": lax.rem(me + step, rows)}, device_id_type=MESH
        )
    pl.semaphore_signal(barrier, inc=1, device_id={"chan": chan_peer}, device_id_type=MESH)
    pl.semaphore_wait(barrier, rows)

    def slot_copy(ref, slot, level, ssem, target):
        return remote(
            ref, wbuf.at[slot, level], ssem, gather_recv.at[level, slot], {"rows": target}
        )

    order = list(range(levels))[::-1]
    for turn, level in enumerate(order):
        for at in range(sources):
            there = own_half + 2 * at
            send(
                there != mine_z,
                slot_copy(
                    own_ref.at[level], own_slot, level, own_send.at[level, at], me + 4 * (there - mine_z)
                ),
            )
        if turn == 0:
            send(None, remote(maps.at[0], maps.at[1], maps_ssem, maps_rsem, {"rows": twin}))

    def flat():
        return f_ref[...].reshape(pixels, depth)

    local = jnp.zeros((8, depth), F32)
    for row in range(strip):
        block = f_ref[row].astype(F32).reshape(cols // 8, 8, depth)
        local = local + jnp.sum(block, axis=0)
    local = jnp.broadcast_to(jnp.sum(local, axis=0, keepdims=True), (8, depth))
    pool_send[0] = jnp.dot(
        local, pool_ref[...].astype(F32), precision=lax.Precision.HIGHEST, preferred_element_type=F32
    )
    peers = ({"chan": chan_peer}, {"rows": core_peer}, {"rows": y_peer})

    def pool_round(turn):
        send(
            None,
            remote(
                pool_send.at[turn], pool_recv.at[turn], pool_ssem.at[turn], pool_rsem.at[turn], peers[turn]
            ),
        )

    def pool_add(turn):
        arrive(None, pool_recv.at[turn], pool_rsem.at[turn], pool_ssem.at[turn])
        pool_send[turn + 1] = pool_send[turn] + pool_recv[turn]

    def merge(slot, value):
        merged[slot] = value.astype(BF16).reshape(strip, cols, width)
        start = pl.multiple_of(chan_peer * (cols - window), 16)
        send(
            None,
            remote(
                merged.at[slot, :, pl.ds(start, window), :],
                chan_recv.at[slot],
                chan_ssem.at[slot],
                chan_rsem.at[slot],
                {"chan": chan_peer},
            ),
        )

    def project(slot, first):
        arrive(None, chan_recv.at[slot], chan_rsem.at[slot], chan_ssem.at[slot])
        start = pl.multiple_of(chan * (cols - window), 16)
        value = merged[slot, :, pl.ds(start, window), :].astype(F32) + chan_recv[slot].astype(F32)
        value = jax.nn.relu(value + branch_bias_ref[slot : slot + 1, :].reshape(1, 1, width))
        value = value.astype(BF16).reshape(strip * window, width)
        term = jnp.dot(
            value, proj_ref[slot * width : (slot + 1) * width, :], preferred_element_type=F32
        )
        if first:
            total[...] = term
        else:
            total[...] += term

    def shift_level(level, which):
        spacing = RATE * (level + 1)

        @pl.loop(0, strip)
        def _(row):
            pos = lax.broadcasted_iota(jnp.int32, (cols, depth), 0)
            value = maps[which, row].astype(F32)
            before = jnp.where(pos < spacing, 0.0, pltpu.roll(value, spacing, 0))
            after = jnp.where(pos >= cols - spacing, 0.0, pltpu.roll(value, cols - spacing, 0))
            shifted[level, 0, which, row] = before.astype(BF16)
            shifted[level, 1, which, row] = after.astype(BF16)

    def mapped_low(value):
        return jax.nn.relu(
            jnp.dot(value, low_weight_ref[...], preferred_element_type=F32) + low_bias_ref[...]
        )

    @pl.loop(0, fine_rows)
    def _(row):
        first = low_ref[row, 0:16, :].astype(F32)
        last = low_ref[row, fine_cols - 16 : fine_cols, :].astype(F32)
        low_edge[pl.ds(row, 1), :] = jnp.where(chan == 0, last[15:16], first[0:1])

    low_send[...] = mapped_low(low_edge[...].astype(BF16))
    send(
        None,
        remote(low_send, low_recv, low_ssem.at[0], low_rsem.at[0], {"chan": chan_peer}),
    )

    pool_round(0)
    merge(0, jnp.dot(flat(), one_ref[...], preferred_element_type=F32))
    pool_add(0)
    pool_round(1)
    shift_level(order[0], 0)
    pool_add(1)
    pool_round(2)

    arrive(None, low_recv, low_rsem.at[0], low_ssem.at[0])

    @pl.loop(0, fine_rows)
    def _(row):
        value = mapped_low(low_ref[row])
        pos = lax.broadcasted_iota(jnp.int32, (fine_cols, packed), 0)
        lane = lax.broadcasted_iota(jnp.int32, (fine_cols, packed), 1)
        outer = low_recv[pl.ds(row, 1), :]
        left = jnp.where(chan == 0, 0.0, outer)
        right = jnp.where(chan == 0, outer, 0.0)
        before = jnp.where(pos == 0, left, pltpu.roll(value, 1, 0))
        after = jnp.where(pos == fine_cols - 1, right, pltpu.roll(value, fine_cols - 1, 0))
        value = jnp.where(lane < low_width, before, jnp.where(lane < 2 * low_width, value, after))
        low_out_ref[row + 1] = value.astype(BF16)

    low_rows_send[0] = low_out_ref[1]
    low_rows_send[1] = low_out_ref[fine_rows]
    for at, offset in enumerate((-1, 1)):
        send(
            (me + offset >= 0) & (me + offset < rows),
            remote(
                low_rows_send.at[at],
                low_rows_recv.at[at],
                low_ssem.at[1 + at],
                low_rsem.at[1 + at],
                {"rows": me + offset},
            ),
        )
    for level in order[1:]:
        shift_level(level, 0)
    pool_add(2)
    pool_line[mine_z] = pool_send[3]
    for step in range(1, lines):
        for at, sign in enumerate((1, -1)):
            there = mine_z + sign * step
            cond = (there >= 0) & (there < lines)
            send(
                cond,
                remote(
                    pool_send.at[3],
                    pool_line.at[mine_z],
                    pool_ssem.at[3 + 2 * (step - 1) + at],
                    pool_rsem.at[3 + mine_z],
                    {"rows": me + 4 * sign * step},
                ),
            )
    project(0, True)

    def gather_level(level):
        count = [0]

        def forward(slot, target):
            ssem = gather_send.at[level, count[0]]
            count[0] += 1
            send(None, slot_copy(wbuf.at[slot, level], slot, level, ssem, target))

        def here(cond, slot):
            arrive(cond, wbuf.at[slot, level], gather_recv.at[level, slot], gather_send.at[level, 0])

        near = [
            jnp.where(mine_z < sources, at, sources - 1 - at) * 4 for at in range(sources)
        ]
        for place in near:
            slot = place + 2 * mine_y + mine_c
            here((half != own_half) | (slot != own_slot), slot)
            forward(slot, y_peer)
            forward(slot, core_peer)
        for place in near:
            slot = place + 2 * (1 - mine_y) + mine_c
            here(None, slot)
            forward(slot, core_peer)
        for place in near:
            for y in range(2):
                here(None, place + 2 * y + 1 - mine_c)

    def row_copies(level):
        hop, remain = divmod(RATE * (level + 1), strip)
        found = []
        if remain < strip:
            found.append((0, hop, 0, remain, strip - remain))
            found.append((2, -hop, remain, 0, strip - remain))
        if remain > 0:
            found.append((0, hop + 1, strip - remain, 0, remain))
            found.append((2, -hop - 1, 0, strip - remain, remain))
        return found

    def compute_strip(level, which):
        def weight(tap):
            return wbuf[:, level, tap].reshape(part, depth)

        outer, centre = None, None
        for across in range(3):
            side = maps[which] if across == 1 else shifted[level, across // 2, which]
            side = side.reshape(pixels, depth)
            pair = jnp.concatenate([weight(across), weight(6 + across)], axis=0)
            term = dot_t(side, pair)
            outer = term if outer is None else outer + term
            term = dot_t(side, weight(3 + across))
            centre = term if centre is None else centre + term
        row_send[level, which, 0] = outer[:, :part].astype(BF16).reshape(strip, cols, part)
        row_send[level, which, 2] = outer[:, part:].astype(BF16).reshape(strip, cols, part)
        centre = centre.astype(BF16).reshape(strip, cols, part)
        if which == 0:
            row_recv[level, 1, :, :, lanes] = centre
        else:
            row_send[level, which, 1] = centre

    def send_strip(level, which):
        base = me if which == 0 else twin
        for index, (down, offset, first, into, count) in enumerate(row_copies(level)):
            there = base + offset
            inside = (there >= 0) & (there < rows)
            source = row_send.at[level, which, down, pl.ds(first, count)]
            target = row_recv.at[level, down, pl.ds(into, count), :, lanes]
            rsem = row_rsem.at[level, index, half]
            away = remote(source, target, row_ssem.at[level, index, which], rsem, {"rows": there})
            if which == 1 and abs(offset) == 4:
                home = pltpu.make_async_copy(source, target, rsem)
                pl.when(there == me)(home.start)
                send(inside & (there != me), away)
            else:
                send(inside, away)
        if which == 1:
            send(
                None,
                remote(
                    row_send.at[level, 1, 1],
                    row_recv.at[level, 1, :, :, lanes],
                    row_ssem.at[level, 4, 1],
                    row_rsem.at[level, 4, half],
                    {"rows": twin},
                ),
            )

    def compute_level(level):
        for which in (1, 0):
            compute_strip(level, which)
            send_strip(level, which)

    def finish_level(level):
        for index, (down, offset, first, into, count) in enumerate(row_copies(level)):
            cond = (me - offset >= 0) & (me - offset < rows)
            for side in range(2):
                arrive(
                    cond,
                    row_recv.at[level, down, pl.ds(into, count), :, pl.ds(side * part, part)],
                    row_rsem.at[level, index, side],
                    row_ssem.at[level, index, 0],
                )
        others = pl.ds(pl.multiple_of((1 - half) * part, part), part)
        arrive(
            None, row_recv.at[level, 1, :, :, others], row_rsem.at[level, 4, 1 - half], row_ssem.at[level, 4, 0]
        )
        value = row_recv[level, 0].astype(F32) + row_recv[level, 1].astype(F32)
        merge(level + 1, value + row_recv[level, 2].astype(F32))

    for turn, level in enumerate(order):
        gather_level(level)
        if turn == 0:
            arrive(None, maps.at[1], maps_rsem, maps_ssem)
            for each in order:
                shift_level(each, 1)
        compute_level(level)
        if turn >= 1:
            finish_level(order[turn - 1])
        if turn >= 2:
            project(order[turn - 2] + 1, False)

    for at, (offset, place) in enumerate(((-1, fine_rows + 1), (1, 0))):
        cond = (me - offset >= 0) & (me - offset < rows)
        arrive(cond, low_rows_recv.at[at], low_rsem.at[1 + at], low_ssem.at[1 + at])
        low_out_ref[place] = low_rows_recv[at]

    for step in range(1, lines):
        for sign in (1, -1):
            there = mine_z + sign * step
            cond = (there >= 0) & (there < lines)
            arrive(cond, pool_line.at[there], pool_rsem.at[3 + there], pool_ssem.at[0])
    pooled = pool_line[0]
    for line in range(1, lines):
        pooled = pooled + pool_line[line]
    pooled = pooled * (1.0 / (rows * pixels))
    pooled = jax.nn.relu(pooled + branch_bias_ref[4:5, :]).astype(BF16)
    constant = jnp.dot(pooled, proj_ref[4 * width :, :], preferred_element_type=F32)
    constant = constant[0:1, :] + proj_bias_ref[...]

    finish_level(order[-1])
    for level in order[-2:]:
        project(level + 1, False)

    value = jax.nn.relu(total[...] + constant).astype(BF16).reshape(strip, window, width)
    context[...] = value
    out_ref[1 : strip + 1] = value
    for at, (row, offset) in enumerate(((0, -1), (strip - 1, 1))):
        cond = (me + offset >= 0) & (me + offset < rows)
        send(
            cond,
            remote(context.at[row], halo.at[at], halo_ssem.at[at], halo_rsem.at[at], {"rows": me + offset}),
        )
    for at, (row, offset) in enumerate(((0, -1), (strip - 1, 1))):
        place = strip + 1 if at == 0 else 0
        edge = strip - 1 if at == 0 else 0
        cond = (me - offset >= 0) & (me - offset < rows)
        arrive(cond, halo.at[at], halo_rsem.at[at], halo_ssem.at[at])

        @pl.when(cond)
        def _():
            out_ref[place] = halo[at]

        @pl.when(jnp.logical_not(cond))
        def _():
            out_ref[place] = context[edge]

    for cond, copy in pending:
        if cond is None:
            copy.wait_send()
        else:
            pl.when(cond)(copy.wait_send)


def pyramid(features, w_one, w_rate, w_pool, b_branch, w_proj, b_proj, low_features, w_low, b_low):
    strip, cols, depth = features.shape
    levels, taps, shard = w_rate.shape[0], w_rate.shape[1], w_rate.shape[3]
    width = w_one.shape[1]
    rows = lax.axis_size("rows")
    lines = rows // 4
    window = cols // 2 + 16
    pixels = strip * cols
    own = jnp.swapaxes(w_rate, 2, 3)
    sources = lines // 2
    fine_rows, fine_cols, low_depth = low_features.shape
    low_width = w_low.shape[1]
    packed = pl.cdiv(3 * low_width, 128) * 128
    rest = packed - 3 * low_width
    low_weight = jnp.pad(jnp.concatenate([w_low] * 3, axis=1), ((0, 0), (0, rest)))
    low_bias = jnp.pad(jnp.concatenate([b_low] * 3), (0, rest))[None, :]
    dma = pltpu.SemaphoreType.DMA
    vmem = pl.BlockSpec(memory_space=pltpu.VMEM)
    return pl.pallas_call(
        lambda *refs: pyramid_kernel((rows, lines, window, low_width), *refs),
        out_shape=(
            jax.ShapeDtypeStruct((strip + 2, window, width), BF16),
            jax.ShapeDtypeStruct((fine_rows + 2, fine_cols, packed), BF16),
        ),
        in_specs=[vmem] * 10,
        out_specs=(vmem, vmem),
        scratch_shapes=[
            pltpu.VMEM((rows // 2, levels, taps, shard, depth), BF16),
            pltpu.VMEM((2, strip, cols, depth), BF16),
            pltpu.VMEM((levels, 2, 2, strip, cols, depth), BF16),
            pltpu.VMEM((levels, 2, 3, strip, cols, width // 2), BF16),
            pltpu.VMEM((levels, 3, strip, cols, width), BF16),
            pltpu.VMEM((levels + 1, strip, cols, width), BF16),
            pltpu.VMEM((levels + 1, strip, window, width), BF16),
            pltpu.VMEM((strip * window, width), F32),
            pltpu.VMEM((strip, window, width), BF16),
            pltpu.VMEM((2, window, width), BF16),
            pltpu.VMEM((4, 8, width), F32),
            pltpu.VMEM((3, 8, width), F32),
            pltpu.VMEM((lines, 8, width), F32),
            dma((levels, sources)),
            dma((levels, 3 * sources)),
            dma((levels, rows // 2)),
            dma((levels, 5, 2)),
            dma((levels, 5, 2)),
            dma((levels + 1,)),
            dma((levels + 1,)),
            dma((2,)),
            dma((2,)),
            dma((3 + 2 * lines,)),
            dma((3 + lines,)),
            dma,
            dma,
            pltpu.VMEM((fine_rows, low_depth), F32),
            pltpu.VMEM((fine_rows, packed), F32),
            pltpu.VMEM((fine_rows, packed), F32),
            pltpu.VMEM((2, fine_cols, packed), BF16),
            pltpu.VMEM((2, fine_cols, packed), BF16),
            dma((3,)),
            dma((3,)),
        ],
        compiler_params=pltpu.CompilerParams(
            collective_id=0, has_side_effects=True, vmem_limit_bytes=56 * 1024 * 1024
        ),
        cost_estimate=pl.CostEstimate(
            flops=2 * pixels * depth * width * (levels * taps + 1),
            bytes_accessed=2 * levels * taps * depth * width,
            transcendentals=0,
        ),
    )(
        features, own, w_one, w_pool, b_branch, w_proj, b_proj[None, :],
        low_features, low_weight, low_bias,
    )


def decoder_kernel(
    strip, coarse_ref, low_ref, blend_ref, up_weight_ref, low_weight_ref, bias_ref, out_ref, fine
):
    at = pl.program_id(0)
    me = lax.axis_index("rows")
    rows = lax.axis_size("rows")
    block, fine_cols, width = out_ref.shape
    fine_rows = fine.shape[0] - 2
    window, depth = coarse_ref.shape[1], coarse_ref.shape[2]

    @pl.when(at == 0)
    def _():
        for row in range(fine_rows + 2):
            pair, phase = divmod(row + 1, 4)
            source = coarse_ref[pair : pair + 2].reshape(2 * window, depth)
            for across in range(3):
                value = jnp.dot(
                    blend_ref[phase, across * fine_cols : (across + 1) * fine_cols, :],
                    source,
                    preferred_element_type=F32,
                )
                if row == 0:
                    value = jnp.where(me == 0, 0.0, value)
                if row == fine_rows + 1:
                    value = jnp.where(me == rows - 1, 0.0, value)
                fine[row, :, across * depth : (across + 1) * depth] = value.astype(BF16)

    total = None
    for down in range(3):
        up = fine[pl.ds(at * block + down, block)].reshape(block * fine_cols, 3 * depth)
        low = low_ref[pl.ds(at * block + down, block)].reshape(block * fine_cols, low_ref.shape[2])
        term = jnp.dot(up, up_weight_ref[down], preferred_element_type=F32)
        term = term + jnp.dot(low, low_weight_ref[down], preferred_element_type=F32)
        total = term if total is None else total + term
    total = jax.nn.relu(total + bias_ref[...])
    out_ref[...] = total.astype(BF16).reshape(block, fine_cols, width)


def blend_matrices(half, window, chan_index):
    fine_cols = 4 * half
    shape = (4, 3, fine_cols, 2, window)
    phase, across, pos, lower, col = (lax.broadcasted_iota(jnp.int32, shape, d) for d in range(5))
    place = pos + across - 1
    pair, col_phase = (place + 2) // 4, (place + 2) % 4
    first = jnp.clip(chan_index * half + pair - 1, 0, 2 * half - 1) - chan_index * (2 * half - window)
    second = jnp.clip(chan_index * half + pair, 0, 2 * half - 1) - chan_index * (2 * half - window)
    col_upper = 0.875 - 0.25 * col_phase.astype(F32)
    factor = jnp.where(col == first, col_upper, 0.0) + jnp.where(col == second, 1.0 - col_upper, 0.0)
    row_upper = 0.875 - 0.25 * phase.astype(F32)
    factor = factor * jnp.where(lower == 0, row_upper, 1.0 - row_upper)
    whole = chan_index * fine_cols + place
    factor = jnp.where((whole >= 0) & (whole < 2 * fine_cols), factor, 0.0)
    return factor.astype(BF16).reshape(4, 3 * fine_cols, 2 * window)


def whole_by_kernels(
    features, low_features, w_one, w_rate, w_pool, b_branch, w_proj, b_proj, w_low, b_low,
    w_dec_up, w_dec_low, b_dec,
):
    strip, cols = features.shape[0], features.shape[1]
    fine_rows, fine_cols = low_features.shape[0], low_features.shape[1]
    depth, width = w_dec_up.shape[1], w_dec_up.shape[2]
    chan_index = lax.axis_index("chan")
    half = cols // 2
    padded, low_packed = pyramid(
        features, w_one, w_rate, w_pool, b_branch, w_proj, b_proj, low_features, w_low, b_low
    )
    window, packed = padded.shape[1], low_packed.shape[2]
    context = jnp.where(chan_index == 0, padded[1:-1, :half], padded[1:-1, window - half :])
    up_weight = w_dec_up.reshape(3, 3 * depth, width)
    low_weight = w_dec_low.reshape(3, -1, width)
    low_weight = jnp.pad(low_weight, ((0, 0), (0, packed - low_weight.shape[1]), (0, 0)))
    blend = blend_matrices(half, window, chan_index)
    whole = pl.BlockSpec(memory_space=pltpu.VMEM)
    block = 4
    pixels = fine_rows * fine_cols
    decoded = pl.pallas_call(
        lambda *refs: decoder_kernel(strip, *refs),
        out_shape=jax.ShapeDtypeStruct((fine_rows, fine_cols, width), BF16),
        grid=(fine_rows // block,),
        in_specs=[whole] * 6,
        out_specs=pl.BlockSpec((block, fine_cols, width), lambda i: (i, 0, 0)),
        scratch_shapes=[pltpu.VMEM((fine_rows + 2, fine_cols, 3 * depth), BF16)],
        compiler_params=pltpu.CompilerParams(vmem_limit_bytes=48 * 1024 * 1024),
        cost_estimate=pl.CostEstimate(
            flops=2 * pixels * width * (9 * depth + 3 * packed),
            bytes_accessed=2 * pixels * (width + packed),
            transcendentals=0,
        ),
    )(padded, low_packed, blend, up_weight, low_weight, b_dec[None, :])
    return context, decoded


def context_by_collectives(features, w_one, w_rate, w_pool, b_branch, w_proj, b_proj):
    strip_rows, map_cols, group_in = features.shape
    branch_width = w_one.shape[1]
    pixel_count = strip_rows * map_cols
    rows_index = lax.axis_index("rows")
    rows_count = lax.axis_size("rows")
    chan_index = lax.axis_index("chan")
    chan_count = lax.axis_size("chan")
    local_sum = jnp.sum(features, axis=(0, 1), dtype=jnp.float32)
    map_total = strip_rows * rows_count * map_cols
    pool_weight = w_pool.astype(jnp.float32)
    pooled = lax.psum(local_sum, "rows") / map_total
    local_term = jnp.dot(pooled, pool_weight, precision=lax.Precision.HIGHEST)
    pool_pre = lax.psum(local_term, "chan")
    pool_branch = jax.nn.relu(pool_pre + b_branch[4]).astype(jnp.bfloat16)
    head_weight = w_proj[: 4 * branch_width]
    pool_term = jnp.dot(
        pool_branch[None, :], w_proj[4 * branch_width :], preferred_element_type=jnp.float32
    )[0]
    rate_all = lax.all_gather(w_rate, "rows", axis=3, tiled=True)
    rate_outputs = []
    for rate_level in range(3):
        matrix = rate_matrix(features, RATE * (rate_level + 1))
        weight_flat = rate_all[rate_level].reshape(-1, rate_all.shape[3])
        rate_outputs.append(jnp.dot(matrix, weight_flat, preferred_element_type=jnp.float32))
    one_out = jnp.dot(
        features.reshape(pixel_count, group_in), w_one, preferred_element_type=jnp.float32
    )
    partial_value = jnp.concatenate([one_out] + rate_outputs, axis=1).reshape(
        strip_rows, map_cols, 4 * branch_width
    )
    conv_bias = b_branch[:4].reshape(-1)
    summed = lax.psum_scatter(
        partial_value.astype(jnp.bfloat16), "chan", scatter_dimension=2, tiled=True
    ).astype(jnp.float32)
    share_width = summed.shape[2]
    bias_share = lax.dynamic_slice_in_dim(conv_bias, chan_index * share_width, share_width)
    branches = jax.nn.relu(summed + bias_share).astype(jnp.bfloat16)
    weight_share = lax.dynamic_slice_in_dim(head_weight, chan_index * share_width, share_width, 0)
    partial_terms = jnp.dot(
        branches.reshape(-1, share_width), weight_share, preferred_element_type=jnp.float32
    )
    partial_terms = partial_terms.reshape(strip_rows, map_cols, branch_width)
    projected = lax.psum_scatter(
        partial_terms.astype(jnp.bfloat16), "chan", scatter_dimension=1, tiled=True
    ).astype(jnp.float32)
    context = jax.nn.relu(projected + pool_term + b_proj).astype(jnp.bfloat16)
    coarse = padded_2(context, (("rows", 0), ("chan", 1)), 1)
    coarse = edge_copy(coarse, rows_index, rows_count, chan_index, chan_count)
    return context, coarse


def on_device(
    features,
    low_features,
    w_one,
    w_rate,
    w_pool,
    b_branch,
    w_proj,
    b_proj,
    w_low,
    b_low,
    w_dec_up,
    w_dec_low,
    b_dec,
):
    rows_index = lax.axis_index("rows")
    rows_count = lax.axis_size("rows")
    chan_index = lax.axis_index("chan")
    chan_count = lax.axis_size("chan")
    fits = (
        chan_count == 2
        and rows_count % 8 == 0
        and w_one.shape[1] % 256 == 0
        and w_rate.shape[3] % 16 == 0
        and features.shape[1] % 32 == 0
        and features.shape[2] % 128 == 0
        and features.shape[0] % 2 == 0
        and low_features.shape[0] == 4 * features.shape[0]
        and low_features.shape[0] % 16 == 0
        and 2 * low_features.shape[1] == 4 * features.shape[1]
    )
    if fits:
        return whole_by_kernels(
            features, low_features, w_one, w_rate, w_pool, b_branch, w_proj, b_proj, w_low, b_low,
            w_dec_up, w_dec_low, b_dec,
        )
    context, coarse = context_by_collectives(
        features, w_one, w_rate, w_pool, b_branch, w_proj, b_proj
    )
    tile_rows_count = context.shape[0]
    tile_cols_count = context.shape[1]
    fine_rows, fine_cols = (low_features.shape[0], low_features.shape[1])
    low_flat = low_features.reshape(fine_rows * fine_cols, low_features.shape[2])
    low_mapped = jax.nn.relu(
        jnp.dot(low_flat, w_low, preferred_element_type=jnp.float32) + b_low
    ).astype(jnp.bfloat16)
    low_mapped = low_mapped.reshape(fine_rows, fine_cols, -1)
    coarse = coarse.astype(jnp.float32)
    upsampled = blend_axis(coarse, 0)[1 : 4 * tile_rows_count + 3]
    upsampled = blend_axis(upsampled, 1)[:, 1 : 4 * tile_cols_count + 3]
    ext_rows, ext_cols = (upsampled.shape[0], upsampled.shape[1])
    row_pos = lax.broadcasted_iota(jnp.int32, (ext_rows, 1, 1), 0)
    col_pos = lax.broadcasted_iota(jnp.int32, (1, ext_cols, 1), 1)
    inside = ((row_pos > 0) | (rows_index > 0)) & (
        (row_pos < ext_rows - 1) | (rows_index < rows_count - 1)
    )
    inside = (
        inside
        & ((col_pos > 0) | (chan_index > 0))
        & ((col_pos < ext_cols - 1) | (chan_index < chan_count - 1))
    )
    up_pad = jnp.where(inside, upsampled, 0.0).astype(jnp.bfloat16)
    low_pad = padded_2(low_mapped, (("rows", 0), ("chan", 1)), 1)
    up_taps = tap_matrix(up_pad, fine_rows, fine_cols)
    low_taps = tap_matrix(low_pad, fine_rows, fine_cols)
    mixed = jnp.dot(
        up_taps, w_dec_up.reshape(-1, w_dec_up.shape[2]), preferred_element_type=jnp.float32
    )
    mixed = mixed + jnp.dot(
        low_taps, w_dec_low.reshape(-1, w_dec_low.shape[2]), preferred_element_type=jnp.float32
    )
    decoded = jax.nn.relu(mixed + b_dec).astype(jnp.bfloat16).reshape(fine_rows, fine_cols, -1)
    return (context, decoded)


def solution(mesh):
    in_specs = (
        P("rows", None, "chan"),
        P("rows", "chan", None),
        P("chan", None),
        P(None, None, "chan", "rows"),
        P("chan", None),
        P(),
        P(),
        P(),
        P(),
        P(),
        P(),
        P(),
        P(),
    )
    out_specs = (P("rows", "chan", None), P("rows", "chan", None))
    return jax.shard_map(
        on_device, mesh=mesh, in_specs=in_specs, out_specs=out_specs, check_vma=False
    )
```

```python
import jax
import jax.numpy as jnp
import numpy as np
from jax import lax
from jax.experimental import pallas as pl
from jax.experimental.pallas import tpu as pltpu
from jax.sharding import PartitionSpec as P

RATE = 6


BLEND = (0.875, 0.625, 0.375, 0.125)


def passed_along(block, axis, distance):
    devices = range(lax.axis_size(axis))
    route = [(i - distance, i) for i in devices if i - distance in devices]
    return lax.ppermute(block, axis, route)


def padded_2(array, sides, width):
    for axis, dim in sides:
        devices, length = (lax.axis_size(axis), array.shape[dim])
        up = [(i, (i + 1) % devices) for i in range(devices - 1)]
        down = [(j, i) for i, j in up]
        last = lax.slice_in_dim(array, length - width, length, axis=dim)
        first = lax.slice_in_dim(array, 0, width, axis=dim)
        before = lax.ppermute(last, axis, up)
        after = lax.ppermute(first, axis, down)
        array = jnp.concatenate([before, array, after], axis=dim)
    return array


def move_cols(field, across):
    extent = field.shape[1]
    amount = abs(across)
    padded = jnp.pad(field, ((0, 0), (amount, amount), (0, 0)))
    return padded[:, amount + across : amount + across + extent]


def fetch_rows(features, offset):
    hop_count, remain = divmod(offset, features.shape[0])
    upper_part = features[remain:]
    upper_part = passed_along(upper_part, "rows", -hop_count)
    if remain == 0:
        return upper_part
    lower_part = features[:remain]
    lower_part = passed_along(lower_part, "rows", -hop_count - 1)
    return jnp.concatenate([upper_part, lower_part], axis=0)


def rate_matrix(features, spacing):
    sources = (fetch_rows(features, -spacing), features, fetch_rows(features, spacing))
    pieces = [
        move_cols(source, (col_step - 1) * spacing) for source in sources for col_step in range(3)
    ]
    stacked = jnp.concatenate(pieces, axis=2)
    return stacked.reshape(-1, stacked.shape[2])


def blend_axis(field, axis_pos):
    count_in = field.shape[axis_pos]
    lower_half = lax.slice_in_dim(field, 0, count_in - 1, axis=axis_pos)
    upper_half = lax.slice_in_dim(field, 1, count_in, axis=axis_pos)
    blended = jnp.stack(
        [factor * lower_half + (1.0 - factor) * upper_half for factor in BLEND], axis=axis_pos + 1
    )
    target = list(lower_half.shape)
    target[axis_pos] = 4 * (count_in - 1)
    return blended.reshape(target)


def edge_copy(padded, rows_index, rows_count, chan_index, chan_count):
    top_row = jnp.where(rows_index == 0, padded[1:2], padded[0:1])
    bottom_row = jnp.where(rows_index == rows_count - 1, padded[-2:-1], padded[-1:])
    padded = jnp.concatenate([top_row, padded[1:-1], bottom_row], axis=0)
    left_col = jnp.where(chan_index == 0, padded[:, 1:2], padded[:, 0:1])
    right_col = jnp.where(chan_index == chan_count - 1, padded[:, -2:-1], padded[:, -1:])
    return jnp.concatenate([left_col, padded[:, 1:-1], right_col], axis=1)


def tap_matrix(padded, out_rows, out_cols):
    pieces = [
        padded[row_step : row_step + out_rows, col_step : col_step + out_cols]
        for row_step in range(3)
        for col_step in range(3)
    ]
    stacked = jnp.concatenate(pieces, axis=2)
    return stacked.reshape(out_rows * out_cols, -1)


F32 = jnp.float32
BF16 = jnp.bfloat16
MESH = pl.DeviceIdType.MESH


def dot_t(lhs, rhs):
    return lax.dot_general(lhs, rhs, (((1,), (1,)), ((), ())), preferred_element_type=F32)


def pyramid_kernel(
    geometry,
    f_ref, own_ref, one_ref, pool_ref, branch_bias_ref, proj_ref, proj_bias_ref,
    low_ref, low_weight_ref, low_bias_ref,
    out_ref, low_out_ref,
    wbuf, maps, shifted, row_send, row_recv, merged, chan_recv, total, context, halo,
    pool_send, pool_recv, pool_line,
    own_send, gather_send, gather_recv, row_ssem, row_rsem, chan_ssem, chan_rsem, halo_ssem, halo_rsem,
    pool_ssem, pool_rsem,
    maps_ssem, maps_rsem, low_edge, low_send, low_recv, low_rows_send, low_rows_recv, low_ssem, low_rsem,
):
    rows, lines, window, low_width = geometry
    fine_rows, fine_cols, low_depth = low_ref.shape
    packed = low_weight_ref.shape[1]
    strip, cols, depth = f_ref.shape
    width = one_ref.shape[1]
    pixels = strip * cols
    me = lax.axis_index("rows")
    chan = lax.axis_index("chan")
    mine_z = me // 4
    mine_y = (me // 2) % 2
    mine_c = me % 2
    half = mine_z % 2
    twin = me + 4 - 8 * half
    sources = lines // 2
    own_half = mine_z // sources
    own_slot = me - own_half * (rows // 2)
    part = width // 2
    lanes = pl.ds(pl.multiple_of(half * part, part), part)
    core_peer = me + 1 - 2 * (me % 2)
    y_peer = me + 2 - 4 * mine_y
    chan_peer = 1 - chan
    levels = own_ref.shape[0]
    pending = []

    def remote(src, dst, ssem, rsem, device):
        return pltpu.make_async_remote_copy(
            src_ref=src, dst_ref=dst, send_sem=ssem, recv_sem=rsem, device_id=device, device_id_type=MESH
        )

    def send(cond, copy):
        if cond is None:
            copy.start()
        else:
            pl.when(cond)(copy.start)
        pending.append((cond, copy))

    def arrive(cond, ref, rsem, ssem):
        copy = remote(ref, ref, ssem, rsem, {"chan": chan_peer})
        if cond is None:
            copy.wait_recv()
        else:
            pl.when(cond)(copy.wait_recv)

    row_recv[...] = jnp.zeros_like(row_recv)
    low_rows_recv[...] = jnp.zeros_like(low_rows_recv)
    maps[0] = f_ref[...]

    @pl.when(own_half == half)
    def _():
        wbuf[own_slot] = own_ref[...]


    barrier = pltpu.get_barrier_semaphore()
    for step in range(1, rows):
        pl.semaphore_signal(
            barrier, inc=1, device_id={"rows": lax.rem(me + step, rows)}, device_id_type=MESH
        )
    pl.semaphore_signal(barrier, inc=1, device_id={"chan": chan_peer}, device_id_type=MESH)
    pl.semaphore_wait(barrier, rows)

    def slot_copy(ref, slot, level, ssem, target):
        return remote(
            ref, wbuf.at[slot, level], ssem, gather_recv.at[level, slot], {"rows": target}
        )

    order = list(range(levels))[::-1]
    for level in order:
        for at in range(sources):
            there = own_half + 2 * at
            send(
                there != mine_z,
                slot_copy(
                    own_ref.at[level], own_slot, level, own_send.at[level, at], me + 4 * (there - mine_z)
                ),
            )
    send(None, remote(maps.at[0], maps.at[1], maps_ssem, maps_rsem, {"rows": twin}))

    def flat():
        return f_ref[...].reshape(pixels, depth)

    peers = ({"chan": chan_peer}, {"rows": core_peer}, {"rows": y_peer})

    def pool_start():
        local = jnp.zeros((8, depth), F32)
        for row in range(strip):
            block = f_ref[row].astype(F32).reshape(cols // 8, 8, depth)
            local = local + jnp.sum(block, axis=0)
        local = jnp.broadcast_to(jnp.sum(local, axis=0, keepdims=True), (8, depth))
        pool_send[0] = jnp.dot(
            local, pool_ref[...].astype(F32), precision=lax.Precision.HIGHEST, preferred_element_type=F32
        )
        pool_round(0)

    def pool_round(turn):
        send(
            None,
            remote(
                pool_send.at[turn], pool_recv.at[turn], pool_ssem.at[turn], pool_rsem.at[turn], peers[turn]
            ),
        )

    def pool_add(turn):
        arrive(None, pool_recv.at[turn], pool_rsem.at[turn], pool_ssem.at[turn])
        pool_send[turn + 1] = pool_send[turn] + pool_recv[turn]

    def merge(slot, value):
        merged[slot] = value.astype(BF16).reshape(strip, cols, width)
        start = pl.multiple_of(chan_peer * (cols - window), 16)
        send(
            None,
            remote(
                merged.at[slot, :, pl.ds(start, window), :],
                chan_recv.at[slot],
                chan_ssem.at[slot],
                chan_rsem.at[slot],
                {"chan": chan_peer},
            ),
        )

    def project(slot, first):
        arrive(None, chan_recv.at[slot], chan_rsem.at[slot], chan_ssem.at[slot])
        start = pl.multiple_of(chan * (cols - window), 16)
        value = merged[slot, :, pl.ds(start, window), :].astype(F32) + chan_recv[slot].astype(F32)
        value = jax.nn.relu(value + branch_bias_ref[slot : slot + 1, :].reshape(1, 1, width))
        value = value.astype(BF16).reshape(strip * window, width)
        term = jnp.dot(
            value, proj_ref[slot * width : (slot + 1) * width, :], preferred_element_type=F32
        )
        if first:
            total[...] = term
        else:
            total[...] += term

    def shift_level(level, which):
        spacing = RATE * (level + 1)

        @pl.loop(0, strip)
        def _(row):
            pos = lax.broadcasted_iota(jnp.int32, (cols, depth), 0)
            value = maps[which, row].astype(F32)
            before = jnp.where(pos < spacing, 0.0, pltpu.roll(value, spacing, 0))
            after = jnp.where(pos >= cols - spacing, 0.0, pltpu.roll(value, cols - spacing, 0))
            shifted[level, 0, which, row] = before.astype(BF16)
            shifted[level, 1, which, row] = after.astype(BF16)

    def mapped_low(value):
        return jax.nn.relu(
            jnp.dot(value, low_weight_ref[...], preferred_element_type=F32) + low_bias_ref[...]
        )

    def low_edges():
        @pl.loop(0, fine_rows)
        def _(row):
            first = low_ref[row, 0:16, :].astype(F32)
            last = low_ref[row, fine_cols - 16 : fine_cols, :].astype(F32)
            low_edge[pl.ds(row, 1), :] = jnp.where(chan == 0, last[15:16], first[0:1])

        low_send[...] = mapped_low(low_edge[...].astype(BF16))
        send(
            None,
            remote(low_send, low_recv, low_ssem.at[0], low_rsem.at[0], {"chan": chan_peer}),
        )

    def low_maps():
        arrive(None, low_recv, low_rsem.at[0], low_ssem.at[0])

        @pl.loop(0, fine_rows)
        def _(row):
            value = mapped_low(low_ref[row])
            pos = lax.broadcasted_iota(jnp.int32, (fine_cols, packed), 0)
            lane = lax.broadcasted_iota(jnp.int32, (fine_cols, packed), 1)
            outer = low_recv[pl.ds(row, 1), :]
            left = jnp.where(chan == 0, 0.0, outer)
            right = jnp.where(chan == 0, outer, 0.0)
            before = jnp.where(pos == 0, left, pltpu.roll(value, 1, 0))
            after = jnp.where(pos == fine_cols - 1, right, pltpu.roll(value, fine_cols - 1, 0))
            value = jnp.where(lane < low_width, before, jnp.where(lane < 2 * low_width, value, after))
            low_out_ref[row + 1] = value.astype(BF16)

        low_rows_send[0] = low_out_ref[1]
        low_rows_send[1] = low_out_ref[fine_rows]
        for at, offset in enumerate((-1, 1)):
            send(
                (me + offset >= 0) & (me + offset < rows),
                remote(
                    low_rows_send.at[at],
                    low_rows_recv.at[at],
                    low_ssem.at[1 + at],
                    low_rsem.at[1 + at],
                    {"rows": me + offset},
                ),
            )

    def pool_lines():
        pool_line[mine_z] = pool_send[3]
        for step in range(1, lines):
            for at, sign in enumerate((1, -1)):
                there = mine_z + sign * step
                cond = (there >= 0) & (there < lines)
                send(
                    cond,
                    remote(
                        pool_send.at[3],
                        pool_line.at[mine_z],
                        pool_ssem.at[3 + 2 * (step - 1) + at],
                        pool_rsem.at[3 + mine_z],
                        {"rows": me + 4 * sign * step},
                    ),
                )

    near = [jnp.where(mine_z < sources, at, sources - 1 - at) * 4 for at in range(sources)]

    def forward(slot, level, index, target):
        send(
            None,
            slot_copy(wbuf.at[slot, level], slot, level, gather_send.at[level, index], target),
        )

    def here(cond, slot, level):
        arrive(cond, wbuf.at[slot, level], gather_recv.at[level, slot], gather_send.at[level, 0])

    def own_column(level):
        for at, place in enumerate(near):
            slot = place + 2 * mine_y + mine_c
            here((half != own_half) | (slot != own_slot), slot, level)
            forward(slot, level, 2 * at, y_peer)
            forward(slot, level, 2 * at + 1, core_peer)

    def other_column(level):
        for at, place in enumerate(near):
            slot = place + 2 * (1 - mine_y) + mine_c
            here(None, slot, level)
            forward(slot, level, 2 * sources + at, core_peer)

    def other_core(level):
        for place in near:
            for y in range(2):
                here(None, place + 2 * y + 1 - mine_c, level)

    def row_copies(level):
        hop, remain = divmod(RATE * (level + 1), strip)
        found = []
        if remain < strip:
            found.append((0, hop, 0, remain, strip - remain))
            found.append((2, -hop, remain, 0, strip - remain))
        if remain > 0:
            found.append((0, hop + 1, strip - remain, 0, remain))
            found.append((2, -hop - 1, 0, strip - remain, remain))
        return found

    def compute_strip(level, which):
        def weight(tap):
            return wbuf[:, level, tap].reshape(part, depth)

        outer, centre = None, None
        for across in range(3):
            side = maps[which] if across == 1 else shifted[level, across // 2, which]
            side = side.reshape(pixels, depth)
            pair = jnp.concatenate([weight(across), weight(6 + across)], axis=0)
            term = dot_t(side, pair)
            outer = term if outer is None else outer + term
            term = dot_t(side, weight(3 + across))
            centre = term if centre is None else centre + term
        row_send[level, which, 0] = outer[:, :part].astype(BF16).reshape(strip, cols, part)
        row_send[level, which, 2] = outer[:, part:].astype(BF16).reshape(strip, cols, part)
        centre = centre.astype(BF16).reshape(strip, cols, part)
        if which == 0:
            row_recv[level, 1, :, :, lanes] = centre
        else:
            row_send[level, which, 1] = centre

    def send_strip(level, which):
        base = me if which == 0 else twin
        for index, (down, offset, first, into, count) in enumerate(row_copies(level)):
            there = base + offset
            inside = (there >= 0) & (there < rows)
            source = row_send.at[level, which, down, pl.ds(first, count)]
            target = row_recv.at[level, down, pl.ds(into, count), :, lanes]
            rsem = row_rsem.at[level, index, half]
            away = remote(source, target, row_ssem.at[level, index, which], rsem, {"rows": there})
            if which == 1 and abs(offset) == 4:
                home = pltpu.make_async_copy(source, target, rsem)
                pl.when(there == me)(home.start)
                send(inside & (there != me), away)
            else:
                send(inside, away)
        if which == 1:
            send(
                None,
                remote(
                    row_send.at[level, 1, 1],
                    row_recv.at[level, 1, :, :, lanes],
                    row_ssem.at[level, 4, 1],
                    row_rsem.at[level, 4, half],
                    {"rows": twin},
                ),
            )

    def work(level, which):
        compute_strip(level, which)
        send_strip(level, which)

    def finish_level(level):
        for index, (down, offset, first, into, count) in enumerate(row_copies(level)):
            cond = (me - offset >= 0) & (me - offset < rows)
            for side in range(2):
                arrive(
                    cond,
                    row_recv.at[level, down, pl.ds(into, count), :, pl.ds(side * part, part)],
                    row_rsem.at[level, index, side],
                    row_ssem.at[level, index, 0],
                )
        others = pl.ds(pl.multiple_of((1 - half) * part, part), part)
        arrive(
            None, row_recv.at[level, 1, :, :, others], row_rsem.at[level, 4, 1 - half], row_ssem.at[level, 4, 0]
        )
        value = row_recv[level, 0].astype(F32) + row_recv[level, 1].astype(F32)
        merge(level + 1, value + row_recv[level, 2].astype(F32))

    assert levels == 3
    one, two, three = order
    low_edges()
    pool_start()
    shift_level(one, 0)
    own_column(one)
    merge(0, jnp.dot(flat(), one_ref[...], preferred_element_type=F32))
    pool_add(0)
    pool_round(1)
    shift_level(two, 0)
    own_column(two)
    other_column(one)
    pool_add(1)
    pool_round(2)
    shift_level(three, 0)
    low_maps()
    own_column(three)
    other_core(one)
    other_column(two)
    work(one, 0)
    pool_add(2)
    pool_lines()
    other_core(two)
    other_column(three)
    work(two, 0)
    project(0, True)
    arrive(None, maps.at[1], maps_rsem, maps_ssem)
    shift_level(one, 1)
    work(one, 1)
    shift_level(two, 1)
    work(two, 1)
    finish_level(one)
    shift_level(three, 1)
    other_core(three)
    work(three, 1)
    work(three, 0)
    finish_level(two)
    project(one + 1, False)

    for at, (offset, place) in enumerate(((-1, fine_rows + 1), (1, 0))):
        cond = (me - offset >= 0) & (me - offset < rows)
        arrive(cond, low_rows_recv.at[at], low_rsem.at[1 + at], low_ssem.at[1 + at])
        low_out_ref[place] = low_rows_recv[at]

    for step in range(1, lines):
        for sign in (1, -1):
            there = mine_z + sign * step
            cond = (there >= 0) & (there < lines)
            arrive(cond, pool_line.at[there], pool_rsem.at[3 + there], pool_ssem.at[0])
    pooled = pool_line[0]
    for line in range(1, lines):
        pooled = pooled + pool_line[line]
    pooled = pooled * (1.0 / (rows * pixels))
    pooled = jax.nn.relu(pooled + branch_bias_ref[4:5, :]).astype(BF16)
    constant = jnp.dot(pooled, proj_ref[4 * width :, :], preferred_element_type=F32)
    constant = constant[0:1, :] + proj_bias_ref[...]

    project(two + 1, False)
    finish_level(three)
    project(three + 1, False)

    value = jax.nn.relu(total[...] + constant).astype(BF16).reshape(strip, window, width)
    context[...] = value
    out_ref[1 : strip + 1] = value
    for at, (row, offset) in enumerate(((0, -1), (strip - 1, 1))):
        cond = (me + offset >= 0) & (me + offset < rows)
        send(
            cond,
            remote(context.at[row], halo.at[at], halo_ssem.at[at], halo_rsem.at[at], {"rows": me + offset}),
        )
    for at, (row, offset) in enumerate(((0, -1), (strip - 1, 1))):
        place = strip + 1 if at == 0 else 0
        edge = strip - 1 if at == 0 else 0
        cond = (me - offset >= 0) & (me - offset < rows)
        arrive(cond, halo.at[at], halo_rsem.at[at], halo_ssem.at[at])

        @pl.when(cond)
        def _():
            out_ref[place] = halo[at]

        @pl.when(jnp.logical_not(cond))
        def _():
            out_ref[place] = context[edge]

    for cond, copy in pending:
        if cond is None:
            copy.wait_send()
        else:
            pl.when(cond)(copy.wait_send)


def pyramid(features, w_one, w_rate, w_pool, b_branch, w_proj, b_proj, low_features, w_low, b_low):
    strip, cols, depth = features.shape
    levels, taps, shard = w_rate.shape[0], w_rate.shape[1], w_rate.shape[3]
    width = w_one.shape[1]
    rows = lax.axis_size("rows")
    lines = rows // 4
    window = cols // 2 + 16
    pixels = strip * cols
    own = jnp.swapaxes(w_rate, 2, 3)
    sources = lines // 2
    fine_rows, fine_cols, low_depth = low_features.shape
    low_width = w_low.shape[1]
    packed = pl.cdiv(3 * low_width, 128) * 128
    rest = packed - 3 * low_width
    low_weight = jnp.pad(jnp.concatenate([w_low] * 3, axis=1), ((0, 0), (0, rest)))
    low_bias = jnp.pad(jnp.concatenate([b_low] * 3), (0, rest))[None, :]
    dma = pltpu.SemaphoreType.DMA
    vmem = pl.BlockSpec(memory_space=pltpu.VMEM)
    return pl.pallas_call(
        lambda *refs: pyramid_kernel((rows, lines, window, low_width), *refs),
        out_shape=(
            jax.ShapeDtypeStruct((strip + 2, window, width), BF16),
            jax.ShapeDtypeStruct((fine_rows + 2, fine_cols, packed), BF16),
        ),
        in_specs=[vmem] * 10,
        out_specs=(vmem, vmem),
        scratch_shapes=[
            pltpu.VMEM((rows // 2, levels, taps, shard, depth), BF16),
            pltpu.VMEM((2, strip, cols, depth), BF16),
            pltpu.VMEM((levels, 2, 2, strip, cols, depth), BF16),
            pltpu.VMEM((levels, 2, 3, strip, cols, width // 2), BF16),
            pltpu.VMEM((levels, 3, strip, cols, width), BF16),
            pltpu.VMEM((levels + 1, strip, cols, width), BF16),
            pltpu.VMEM((levels + 1, strip, window, width), BF16),
            pltpu.VMEM((strip * window, width), F32),
            pltpu.VMEM((strip, window, width), BF16),
            pltpu.VMEM((2, window, width), BF16),
            pltpu.VMEM((4, 8, width), F32),
            pltpu.VMEM((3, 8, width), F32),
            pltpu.VMEM((lines, 8, width), F32),
            dma((levels, sources)),
            dma((levels, 3 * sources)),
            dma((levels, rows // 2)),
            dma((levels, 5, 2)),
            dma((levels, 5, 2)),
            dma((levels + 1,)),
            dma((levels + 1,)),
            dma((2,)),
            dma((2,)),
            dma((3 + 2 * lines,)),
            dma((3 + lines,)),
            dma,
            dma,
            pltpu.VMEM((fine_rows, low_depth), F32),
            pltpu.VMEM((fine_rows, packed), F32),
            pltpu.VMEM((fine_rows, packed), F32),
            pltpu.VMEM((2, fine_cols, packed), BF16),
            pltpu.VMEM((2, fine_cols, packed), BF16),
            dma((3,)),
            dma((3,)),
        ],
        compiler_params=pltpu.CompilerParams(
            collective_id=0, has_side_effects=True, vmem_limit_bytes=56 * 1024 * 1024
        ),
        cost_estimate=pl.CostEstimate(
            flops=2 * pixels * depth * width * (levels * taps + 1),
            bytes_accessed=2 * levels * taps * depth * width,
            transcendentals=0,
        ),
    )(
        features, own, w_one, w_pool, b_branch, w_proj, b_proj[None, :],
        low_features, low_weight, low_bias,
    )


def decoder_kernel(
    strip, coarse_ref, low_ref, blend_ref, up_weight_ref, low_weight_ref, bias_ref, out_ref, fine
):
    at = pl.program_id(0)
    me = lax.axis_index("rows")
    rows = lax.axis_size("rows")
    block, fine_cols, width = out_ref.shape
    fine_rows = fine.shape[0] - 2
    window, depth = coarse_ref.shape[1], coarse_ref.shape[2]

    @pl.when(at == 0)
    def _():
        for row in range(fine_rows + 2):
            pair, phase = divmod(row + 1, 4)
            source = coarse_ref[pair : pair + 2].reshape(2 * window, depth)
            for across in range(3):
                value = jnp.dot(
                    blend_ref[phase, across * fine_cols : (across + 1) * fine_cols, :],
                    source,
                    preferred_element_type=F32,
                )
                if row == 0:
                    value = jnp.where(me == 0, 0.0, value)
                if row == fine_rows + 1:
                    value = jnp.where(me == rows - 1, 0.0, value)
                fine[row, :, across * depth : (across + 1) * depth] = value.astype(BF16)

    total = None
    for down in range(3):
        up = fine[pl.ds(at * block + down, block)].reshape(block * fine_cols, 3 * depth)
        low = low_ref[pl.ds(at * block + down, block)].reshape(block * fine_cols, low_ref.shape[2])
        term = jnp.dot(up, up_weight_ref[down], preferred_element_type=F32)
        term = term + jnp.dot(low, low_weight_ref[down], preferred_element_type=F32)
        total = term if total is None else total + term
    total = jax.nn.relu(total + bias_ref[...])
    out_ref[...] = total.astype(BF16).reshape(block, fine_cols, width)


def blend_table(half, window, chan_count):
    fine_cols = 4 * half
    shape = (chan_count, 4, 3, fine_cols, 2, window)
    chan, phase, across, pos, lower, col = np.indices(shape, sparse=True)
    place = pos + across - 1
    pair, col_phase = (place + 2) // 4, (place + 2) % 4
    origin = chan * (chan_count * half - window)
    last = chan_count * half - 1
    first = np.clip(chan * half + pair - 1, 0, last) - origin
    second = np.clip(chan * half + pair, 0, last) - origin
    col_upper = 0.875 - 0.25 * col_phase
    factor = np.where(col == first, col_upper, 0.0) + np.where(col == second, 1.0 - col_upper, 0.0)
    row_upper = 0.875 - 0.25 * phase
    factor = factor * np.where(lower == 0, row_upper, 1.0 - row_upper)
    whole = chan * fine_cols + place
    factor = np.where((whole >= 0) & (whole < chan_count * fine_cols), factor, 0.0)
    return factor.astype(np.float32).astype(BF16).reshape(chan_count, 4, 3 * fine_cols, 2 * window)


def whole_by_kernels(
    features, low_features, w_one, w_rate, w_pool, b_branch, w_proj, b_proj, w_low, b_low,
    w_dec_up, w_dec_low, b_dec,
):
    strip, cols = features.shape[0], features.shape[1]
    fine_rows, fine_cols = low_features.shape[0], low_features.shape[1]
    depth, width = w_dec_up.shape[1], w_dec_up.shape[2]
    chan_index = lax.axis_index("chan")
    half = cols // 2
    padded, low_packed = pyramid(
        features, w_one, w_rate, w_pool, b_branch, w_proj, b_proj, low_features, w_low, b_low
    )
    window, packed = padded.shape[1], low_packed.shape[2]
    context = jnp.where(chan_index == 0, padded[1:-1, :half], padded[1:-1, window - half :])
    up_weight = w_dec_up.reshape(3, 3 * depth, width)
    low_weight = w_dec_low.reshape(3, -1, width)
    low_weight = jnp.pad(low_weight, ((0, 0), (0, packed - low_weight.shape[1]), (0, 0)))
    table = blend_table(half, window, 2)
    blend = jnp.where(chan_index == 0, table[0], table[1])
    whole = pl.BlockSpec(memory_space=pltpu.VMEM)
    block = 4
    pixels = fine_rows * fine_cols
    decoded = pl.pallas_call(
        lambda *refs: decoder_kernel(strip, *refs),
        out_shape=jax.ShapeDtypeStruct((fine_rows, fine_cols, width), BF16),
        grid=(fine_rows // block,),
        in_specs=[whole] * 6,
        out_specs=pl.BlockSpec((block, fine_cols, width), lambda i: (i, 0, 0)),
        scratch_shapes=[pltpu.VMEM((fine_rows + 2, fine_cols, 3 * depth), BF16)],
        compiler_params=pltpu.CompilerParams(vmem_limit_bytes=48 * 1024 * 1024),
        cost_estimate=pl.CostEstimate(
            flops=2 * pixels * width * (9 * depth + 3 * packed),
            bytes_accessed=2 * pixels * (width + packed),
            transcendentals=0,
        ),
    )(padded, low_packed, blend, up_weight, low_weight, b_dec[None, :])
    return context, decoded


def context_by_collectives(features, w_one, w_rate, w_pool, b_branch, w_proj, b_proj):
    strip_rows, map_cols, group_in = features.shape
    branch_width = w_one.shape[1]
    pixel_count = strip_rows * map_cols
    rows_index = lax.axis_index("rows")
    rows_count = lax.axis_size("rows")
    chan_index = lax.axis_index("chan")
    chan_count = lax.axis_size("chan")
    local_sum = jnp.sum(features, axis=(0, 1), dtype=jnp.float32)
    map_total = strip_rows * rows_count * map_cols
    pool_weight = w_pool.astype(jnp.float32)
    pooled = lax.psum(local_sum, "rows") / map_total
    local_term = jnp.dot(pooled, pool_weight, precision=lax.Precision.HIGHEST)
    pool_pre = lax.psum(local_term, "chan")
    pool_branch = jax.nn.relu(pool_pre + b_branch[4]).astype(jnp.bfloat16)
    head_weight = w_proj[: 4 * branch_width]
    pool_term = jnp.dot(
        pool_branch[None, :], w_proj[4 * branch_width :], preferred_element_type=jnp.float32
    )[0]
    rate_all = lax.all_gather(w_rate, "rows", axis=3, tiled=True)
    rate_outputs = []
    for rate_level in range(3):
        matrix = rate_matrix(features, RATE * (rate_level + 1))
        weight_flat = rate_all[rate_level].reshape(-1, rate_all.shape[3])
        rate_outputs.append(jnp.dot(matrix, weight_flat, preferred_element_type=jnp.float32))
    one_out = jnp.dot(
        features.reshape(pixel_count, group_in), w_one, preferred_element_type=jnp.float32
    )
    partial_value = jnp.concatenate([one_out] + rate_outputs, axis=1).reshape(
        strip_rows, map_cols, 4 * branch_width
    )
    conv_bias = b_branch[:4].reshape(-1)
    summed = lax.psum_scatter(
        partial_value.astype(jnp.bfloat16), "chan", scatter_dimension=2, tiled=True
    ).astype(jnp.float32)
    share_width = summed.shape[2]
    bias_share = lax.dynamic_slice_in_dim(conv_bias, chan_index * share_width, share_width)
    branches = jax.nn.relu(summed + bias_share).astype(jnp.bfloat16)
    weight_share = lax.dynamic_slice_in_dim(head_weight, chan_index * share_width, share_width, 0)
    partial_terms = jnp.dot(
        branches.reshape(-1, share_width), weight_share, preferred_element_type=jnp.float32
    )
    partial_terms = partial_terms.reshape(strip_rows, map_cols, branch_width)
    projected = lax.psum_scatter(
        partial_terms.astype(jnp.bfloat16), "chan", scatter_dimension=1, tiled=True
    ).astype(jnp.float32)
    context = jax.nn.relu(projected + pool_term + b_proj).astype(jnp.bfloat16)
    coarse = padded_2(context, (("rows", 0), ("chan", 1)), 1)
    coarse = edge_copy(coarse, rows_index, rows_count, chan_index, chan_count)
    return context, coarse


def on_device(
    features,
    low_features,
    w_one,
    w_rate,
    w_pool,
    b_branch,
    w_proj,
    b_proj,
    w_low,
    b_low,
    w_dec_up,
    w_dec_low,
    b_dec,
):
    rows_index = lax.axis_index("rows")
    rows_count = lax.axis_size("rows")
    chan_index = lax.axis_index("chan")
    chan_count = lax.axis_size("chan")
    fits = (
        chan_count == 2
        and rows_count % 8 == 0
        and w_one.shape[1] % 256 == 0
        and w_rate.shape[3] % 16 == 0
        and features.shape[1] % 32 == 0
        and features.shape[2] % 128 == 0
        and features.shape[0] % 2 == 0
        and low_features.shape[0] == 4 * features.shape[0]
        and low_features.shape[0] % 16 == 0
        and 2 * low_features.shape[1] == 4 * features.shape[1]
    )
    if fits:
        return whole_by_kernels(
            features, low_features, w_one, w_rate, w_pool, b_branch, w_proj, b_proj, w_low, b_low,
            w_dec_up, w_dec_low, b_dec,
        )
    context, coarse = context_by_collectives(
        features, w_one, w_rate, w_pool, b_branch, w_proj, b_proj
    )
    tile_rows_count = context.shape[0]
    tile_cols_count = context.shape[1]
    fine_rows, fine_cols = (low_features.shape[0], low_features.shape[1])
    low_flat = low_features.reshape(fine_rows * fine_cols, low_features.shape[2])
    low_mapped = jax.nn.relu(
        jnp.dot(low_flat, w_low, preferred_element_type=jnp.float32) + b_low
    ).astype(jnp.bfloat16)
    low_mapped = low_mapped.reshape(fine_rows, fine_cols, -1)
    coarse = coarse.astype(jnp.float32)
    upsampled = blend_axis(coarse, 0)[1 : 4 * tile_rows_count + 3]
    upsampled = blend_axis(upsampled, 1)[:, 1 : 4 * tile_cols_count + 3]
    ext_rows, ext_cols = (upsampled.shape[0], upsampled.shape[1])
    row_pos = lax.broadcasted_iota(jnp.int32, (ext_rows, 1, 1), 0)
    col_pos = lax.broadcasted_iota(jnp.int32, (1, ext_cols, 1), 1)
    inside = ((row_pos > 0) | (rows_index > 0)) & (
        (row_pos < ext_rows - 1) | (rows_index < rows_count - 1)
    )
    inside = (
        inside
        & ((col_pos > 0) | (chan_index > 0))
        & ((col_pos < ext_cols - 1) | (chan_index < chan_count - 1))
    )
    up_pad = jnp.where(inside, upsampled, 0.0).astype(jnp.bfloat16)
    low_pad = padded_2(low_mapped, (("rows", 0), ("chan", 1)), 1)
    up_taps = tap_matrix(up_pad, fine_rows, fine_cols)
    low_taps = tap_matrix(low_pad, fine_rows, fine_cols)
    mixed = jnp.dot(
        up_taps, w_dec_up.reshape(-1, w_dec_up.shape[2]), preferred_element_type=jnp.float32
    )
    mixed = mixed + jnp.dot(
        low_taps, w_dec_low.reshape(-1, w_dec_low.shape[2]), preferred_element_type=jnp.float32
    )
    decoded = jax.nn.relu(mixed + b_dec).astype(jnp.bfloat16).reshape(fine_rows, fine_cols, -1)
    return (context, decoded)


def solution(mesh):
    in_specs = (
        P("rows", None, "chan"),
        P("rows", "chan", None),
        P("chan", None),
        P(None, None, "chan", "rows"),
        P("chan", None),
        P(),
        P(),
        P(),
        P(),
        P(),
        P(),
        P(),
        P(),
    )
    out_specs = (P("rows", "chan", None), P("rows", "chan", None))
    return jax.shard_map(
        on_device, mesh=mesh, in_specs=in_specs, out_specs=out_specs, check_vma=False
    )
```

```python
import jax
import jax.numpy as jnp
from jax import lax
from jax.experimental import pallas as pl
from jax.experimental.pallas import tpu as pltpu
from jax.sharding import PartitionSpec as P

RATE = 6


BLEND = (0.875, 0.625, 0.375, 0.125)


def passed_along(block, axis, distance):
    devices = range(lax.axis_size(axis))
    route = [(i - distance, i) for i in devices if i - distance in devices]
    return lax.ppermute(block, axis, route)


def padded_2(array, sides, width):
    for axis, dim in sides:
        devices, length = (lax.axis_size(axis), array.shape[dim])
        up = [(i, (i + 1) % devices) for i in range(devices - 1)]
        down = [(j, i) for i, j in up]
        last = lax.slice_in_dim(array, length - width, length, axis=dim)
        first = lax.slice_in_dim(array, 0, width, axis=dim)
        before = lax.ppermute(last, axis, up)
        after = lax.ppermute(first, axis, down)
        array = jnp.concatenate([before, array, after], axis=dim)
    return array


def move_cols(field, across):
    extent = field.shape[1]
    amount = abs(across)
    padded = jnp.pad(field, ((0, 0), (amount, amount), (0, 0)))
    return padded[:, amount + across : amount + across + extent]


def fetch_rows(features, offset):
    hop_count, remain = divmod(offset, features.shape[0])
    upper_part = features[remain:]
    upper_part = passed_along(upper_part, "rows", -hop_count)
    if remain == 0:
        return upper_part
    lower_part = features[:remain]
    lower_part = passed_along(lower_part, "rows", -hop_count - 1)
    return jnp.concatenate([upper_part, lower_part], axis=0)


def rate_matrix(features, spacing):
    sources = (fetch_rows(features, -spacing), features, fetch_rows(features, spacing))
    pieces = [
        move_cols(source, (col_step - 1) * spacing) for source in sources for col_step in range(3)
    ]
    stacked = jnp.concatenate(pieces, axis=2)
    return stacked.reshape(-1, stacked.shape[2])


def blend_axis(field, axis_pos):
    count_in = field.shape[axis_pos]
    lower_half = lax.slice_in_dim(field, 0, count_in - 1, axis=axis_pos)
    upper_half = lax.slice_in_dim(field, 1, count_in, axis=axis_pos)
    blended = jnp.stack(
        [factor * lower_half + (1.0 - factor) * upper_half for factor in BLEND], axis=axis_pos + 1
    )
    target = list(lower_half.shape)
    target[axis_pos] = 4 * (count_in - 1)
    return blended.reshape(target)


def edge_copy(padded, rows_index, rows_count, chan_index, chan_count):
    top_row = jnp.where(rows_index == 0, padded[1:2], padded[0:1])
    bottom_row = jnp.where(rows_index == rows_count - 1, padded[-2:-1], padded[-1:])
    padded = jnp.concatenate([top_row, padded[1:-1], bottom_row], axis=0)
    left_col = jnp.where(chan_index == 0, padded[:, 1:2], padded[:, 0:1])
    right_col = jnp.where(chan_index == chan_count - 1, padded[:, -2:-1], padded[:, -1:])
    return jnp.concatenate([left_col, padded[:, 1:-1], right_col], axis=1)


def tap_matrix(padded, out_rows, out_cols):
    pieces = [
        padded[row_step : row_step + out_rows, col_step : col_step + out_cols]
        for row_step in range(3)
        for col_step in range(3)
    ]
    stacked = jnp.concatenate(pieces, axis=2)
    return stacked.reshape(out_rows * out_cols, -1)


F32 = jnp.float32
BF16 = jnp.bfloat16
MESH = pl.DeviceIdType.MESH


def dot_t(lhs, rhs):
    return lax.dot_general(lhs, rhs, (((1,), (1,)), ((), ())), preferred_element_type=F32)


def pyramid_kernel(
    geometry,
    f_ref, own_ref, one_ref, pool_ref, branch_bias_ref, proj_ref, proj_bias_ref,
    low_ref, low_weight_ref, low_bias_ref,
    out_ref, low_out_ref,
    wbuf, maps, shifted, row_send, row_recv, merged, chan_recv, total, context, halo,
    pool_send, pool_recv, pool_line,
    own_send, gather_send, gather_recv, row_ssem, row_rsem, chan_ssem, chan_rsem, halo_ssem, halo_rsem,
    pool_ssem, pool_rsem,
    maps_ssem, maps_rsem, low_edge, low_send, low_recv, low_rows_send, low_rows_recv, low_ssem, low_rsem,
):
    rows, lines, window, low_width = geometry
    fine_rows, fine_cols, low_depth = low_ref.shape
    packed = low_weight_ref.shape[1]
    strip, cols, depth = f_ref.shape
    width = one_ref.shape[1]
    pixels = strip * cols
    me = lax.axis_index("rows")
    chan = lax.axis_index("chan")
    mine_z = me // 4
    mine_y = (me // 2) % 2
    mine_c = me % 2
    half = mine_z % 2
    twin = me + 4 - 8 * half
    sources = lines // 2
    own_half = mine_z // sources
    own_slot = me - own_half * (rows // 2)
    part = width // 2
    lanes = pl.ds(pl.multiple_of(half * part, part), part)
    core_peer = me + 1 - 2 * (me % 2)
    y_peer = me + 2 - 4 * mine_y
    chan_peer = 1 - chan
    levels = own_ref.shape[0]
    pending = []

    def remote(src, dst, ssem, rsem, device):
        return pltpu.make_async_remote_copy(
            src_ref=src, dst_ref=dst, send_sem=ssem, recv_sem=rsem, device_id=device, device_id_type=MESH
        )

    def send(cond, copy):
        if cond is None:
            copy.start()
        else:
            pl.when(cond)(copy.start)
        pending.append((cond, copy))

    def arrive(cond, ref, rsem, ssem):
        copy = remote(ref, ref, ssem, rsem, {"chan": chan_peer})
        if cond is None:
            copy.wait_recv()
        else:
            pl.when(cond)(copy.wait_recv)

    row_recv[...] = jnp.zeros_like(row_recv)
    low_rows_recv[...] = jnp.zeros_like(low_rows_recv)
    maps[0] = f_ref[...]

    @pl.when(own_half == half)
    def _():
        wbuf[own_slot] = own_ref[...]


    barrier = pltpu.get_barrier_semaphore()
    for step in range(1, rows):
        pl.semaphore_signal(
            barrier, inc=1, device_id={"rows": lax.rem(me + step, rows)}, device_id_type=MESH
        )
    pl.semaphore_signal(barrier, inc=1, device_id={"chan": chan_peer}, device_id_type=MESH)
    pl.semaphore_wait(barrier, rows)

    def slot_copy(ref, slot, level, ssem, target):
        return remote(
            ref, wbuf.at[slot, level], ssem, gather_recv.at[level, slot], {"rows": target}
        )

    order = list(range(levels))[::-1]
    for turn, level in enumerate(order):
        for at in range(sources):
            there = own_half + 2 * at
            send(
                there != mine_z,
                slot_copy(
                    own_ref.at[level], own_slot, level, own_send.at[level, at], me + 4 * (there - mine_z)
                ),
            )
        if turn == 0:
            send(None, remote(maps.at[0], maps.at[1], maps_ssem, maps_rsem, {"rows": twin}))

    def flat():
        return f_ref[...].reshape(pixels, depth)

    peers = ({"chan": chan_peer}, {"rows": core_peer}, {"rows": y_peer})

    def pool_start():
        local = jnp.zeros((8, depth), F32)
        for row in range(strip):
            block = f_ref[row].astype(F32).reshape(cols // 8, 8, depth)
            local = local + jnp.sum(block, axis=0)
        local = jnp.broadcast_to(jnp.sum(local, axis=0, keepdims=True), (8, depth))
        pool_send[0] = jnp.dot(
            local, pool_ref[...].astype(F32), precision=lax.Precision.HIGHEST, preferred_element_type=F32
        )
        pool_round(0)

    def pool_round(turn):
        send(
            None,
            remote(
                pool_send.at[turn], pool_recv.at[turn], pool_ssem.at[turn], pool_rsem.at[turn], peers[turn]
            ),
        )

    def pool_add(turn):
        arrive(None, pool_recv.at[turn], pool_rsem.at[turn], pool_ssem.at[turn])
        pool_send[turn + 1] = pool_send[turn] + pool_recv[turn]

    def merge(slot, value):
        merged[slot] = value.astype(BF16).reshape(strip, cols, width)
        start = pl.multiple_of(chan_peer * (cols - window), 16)
        send(
            None,
            remote(
                merged.at[slot, :, pl.ds(start, window), :],
                chan_recv.at[slot],
                chan_ssem.at[slot],
                chan_rsem.at[slot],
                {"chan": chan_peer},
            ),
        )

    def project(slot, first):
        arrive(None, chan_recv.at[slot], chan_rsem.at[slot], chan_ssem.at[slot])
        start = pl.multiple_of(chan * (cols - window), 16)
        value = merged[slot, :, pl.ds(start, window), :].astype(F32) + chan_recv[slot].astype(F32)
        value = jax.nn.relu(value + branch_bias_ref[slot : slot + 1, :].reshape(1, 1, width))
        value = value.astype(BF16).reshape(strip * window, width)
        term = jnp.dot(
            value, proj_ref[slot * width : (slot + 1) * width, :], preferred_element_type=F32
        )
        if first:
            total[...] = term
        else:
            total[...] += term

    def shift_level(level, which):
        spacing = RATE * (level + 1)

        @pl.loop(0, strip)
        def _(row):
            pos = lax.broadcasted_iota(jnp.int32, (cols, depth), 0)
            value = maps[which, row].astype(F32)
            before = jnp.where(pos < spacing, 0.0, pltpu.roll(value, spacing, 0))
            after = jnp.where(pos >= cols - spacing, 0.0, pltpu.roll(value, cols - spacing, 0))
            shifted[level, 0, which, row] = before.astype(BF16)
            shifted[level, 1, which, row] = after.astype(BF16)

    def mapped_low(value):
        return jax.nn.relu(
            jnp.dot(value, low_weight_ref[...], preferred_element_type=F32) + low_bias_ref[...]
        )

    def low_edges():
        @pl.loop(0, fine_rows)
        def _(row):
            first = low_ref[row, 0:16, :].astype(F32)
            last = low_ref[row, fine_cols - 16 : fine_cols, :].astype(F32)
            low_edge[pl.ds(row, 1), :] = jnp.where(chan == 0, last[15:16], first[0:1])

        low_send[...] = mapped_low(low_edge[...].astype(BF16))
        send(
            None,
            remote(low_send, low_recv, low_ssem.at[0], low_rsem.at[0], {"chan": chan_peer}),
        )

    def low_maps():
        arrive(None, low_recv, low_rsem.at[0], low_ssem.at[0])

        @pl.loop(0, fine_rows)
        def _(row):
            value = mapped_low(low_ref[row])
            pos = lax.broadcasted_iota(jnp.int32, (fine_cols, packed), 0)
            lane = lax.broadcasted_iota(jnp.int32, (fine_cols, packed), 1)
            outer = low_recv[pl.ds(row, 1), :]
            left = jnp.where(chan == 0, 0.0, outer)
            right = jnp.where(chan == 0, outer, 0.0)
            before = jnp.where(pos == 0, left, pltpu.roll(value, 1, 0))
            after = jnp.where(pos == fine_cols - 1, right, pltpu.roll(value, fine_cols - 1, 0))
            value = jnp.where(lane < low_width, before, jnp.where(lane < 2 * low_width, value, after))
            low_out_ref[row + 1] = value.astype(BF16)

        low_rows_send[0] = low_out_ref[1]
        low_rows_send[1] = low_out_ref[fine_rows]
        for at, offset in enumerate((-1, 1)):
            send(
                (me + offset >= 0) & (me + offset < rows),
                remote(
                    low_rows_send.at[at],
                    low_rows_recv.at[at],
                    low_ssem.at[1 + at],
                    low_rsem.at[1 + at],
                    {"rows": me + offset},
                ),
            )

    def pool_lines():
        pool_line[mine_z] = pool_send[3]
        for step in range(1, lines):
            for at, sign in enumerate((1, -1)):
                there = mine_z + sign * step
                cond = (there >= 0) & (there < lines)
                send(
                    cond,
                    remote(
                        pool_send.at[3],
                        pool_line.at[mine_z],
                        pool_ssem.at[3 + 2 * (step - 1) + at],
                        pool_rsem.at[3 + mine_z],
                        {"rows": me + 4 * sign * step},
                    ),
                )

    near = [jnp.where(mine_z < sources, at, sources - 1 - at) * 4 for at in range(sources)]

    def forward(slot, level, index, target):
        send(
            None,
            slot_copy(wbuf.at[slot, level], slot, level, gather_send.at[level, index], target),
        )

    def here(cond, slot, level):
        arrive(cond, wbuf.at[slot, level], gather_recv.at[level, slot], gather_send.at[level, 0])

    def own_column(level):
        for at, place in enumerate(near):
            slot = place + 2 * mine_y + mine_c
            here((half != own_half) | (slot != own_slot), slot, level)
            forward(slot, level, 2 * at, y_peer)
            forward(slot, level, 2 * at + 1, core_peer)

    def other_column(level):
        for at, place in enumerate(near):
            slot = place + 2 * (1 - mine_y) + mine_c
            here(None, slot, level)
            forward(slot, level, 2 * sources + at, core_peer)

    def other_core(level):
        for place in near:
            for y in range(2):
                here(None, place + 2 * y + 1 - mine_c, level)

    def row_copies(level):
        hop, remain = divmod(RATE * (level + 1), strip)
        found = []
        if remain < strip:
            found.append((0, hop, 0, remain, strip - remain))
            found.append((2, -hop, remain, 0, strip - remain))
        if remain > 0:
            found.append((0, hop + 1, strip - remain, 0, remain))
            found.append((2, -hop - 1, 0, strip - remain, remain))
        return found

    def compute_strip(level, which):
        def weight(tap):
            return wbuf[:, level, tap].reshape(part, depth)

        outer, centre = None, None
        for across in range(3):
            side = maps[which] if across == 1 else shifted[level, across // 2, which]
            side = side.reshape(pixels, depth)
            pair = jnp.concatenate([weight(across), weight(6 + across)], axis=0)
            term = dot_t(side, pair)
            outer = term if outer is None else outer + term
            term = dot_t(side, weight(3 + across))
            centre = term if centre is None else centre + term
        row_send[level, which, 0] = outer[:, :part].astype(BF16).reshape(strip, cols, part)
        row_send[level, which, 2] = outer[:, part:].astype(BF16).reshape(strip, cols, part)
        centre = centre.astype(BF16).reshape(strip, cols, part)
        if which == 0:
            row_recv[level, 1, :, :, lanes] = centre
        else:
            row_send[level, which, 1] = centre

    def send_strip(level, which):
        base = me if which == 0 else twin
        for index, (down, offset, first, into, count) in enumerate(row_copies(level)):
            there = base + offset
            inside = (there >= 0) & (there < rows)
            source = row_send.at[level, which, down, pl.ds(first, count)]
            target = row_recv.at[level, down, pl.ds(into, count), :, lanes]
            rsem = row_rsem.at[level, index, half]
            away = remote(source, target, row_ssem.at[level, index, which], rsem, {"rows": there})
            if which == 1 and abs(offset) == 4:
                home = pltpu.make_async_copy(source, target, rsem)
                pl.when(there == me)(home.start)
                send(inside & (there != me), away)
            else:
                send(inside, away)
        if which == 1:
            send(
                None,
                remote(
                    row_send.at[level, 1, 1],
                    row_recv.at[level, 1, :, :, lanes],
                    row_ssem.at[level, 4, 1],
                    row_rsem.at[level, 4, half],
                    {"rows": twin},
                ),
            )

    def work(level, which):
        compute_strip(level, which)
        send_strip(level, which)

    def finish_level(level):
        for index, (down, offset, first, into, count) in enumerate(row_copies(level)):
            cond = (me - offset >= 0) & (me - offset < rows)
            for side in range(2):
                arrive(
                    cond,
                    row_recv.at[level, down, pl.ds(into, count), :, pl.ds(side * part, part)],
                    row_rsem.at[level, index, side],
                    row_ssem.at[level, index, 0],
                )
        others = pl.ds(pl.multiple_of((1 - half) * part, part), part)
        arrive(
            None, row_recv.at[level, 1, :, :, others], row_rsem.at[level, 4, 1 - half], row_ssem.at[level, 4, 0]
        )
        value = row_recv[level, 0].astype(F32) + row_recv[level, 1].astype(F32)
        merge(level + 1, value + row_recv[level, 2].astype(F32))

    assert levels == 3
    one, two, three = order
    low_edges()
    pool_start()
    shift_level(one, 0)
    own_column(one)
    merge(0, jnp.dot(flat(), one_ref[...], preferred_element_type=F32))
    pool_add(0)
    pool_round(1)
    shift_level(two, 0)
    other_column(one)
    pool_add(1)
    pool_round(2)
    shift_level(three, 0)
    low_maps()
    other_core(one)
    work(one, 0)
    pool_add(2)
    pool_lines()
    arrive(None, maps.at[1], maps_rsem, maps_ssem)
    shift_level(one, 1)
    own_column(two)
    work(one, 1)
    shift_level(two, 1)
    other_column(two)
    project(0, True)
    shift_level(three, 1)
    other_core(two)
    work(two, 1)
    own_column(three)
    work(two, 0)
    other_column(three)
    finish_level(one)
    other_core(three)
    work(three, 1)
    work(three, 0)
    finish_level(two)
    project(one + 1, False)

    for at, (offset, place) in enumerate(((-1, fine_rows + 1), (1, 0))):
        cond = (me - offset >= 0) & (me - offset < rows)
        arrive(cond, low_rows_recv.at[at], low_rsem.at[1 + at], low_ssem.at[1 + at])
        low_out_ref[place] = low_rows_recv[at]

    for step in range(1, lines):
        for sign in (1, -1):
            there = mine_z + sign * step
            cond = (there >= 0) & (there < lines)
            arrive(cond, pool_line.at[there], pool_rsem.at[3 + there], pool_ssem.at[0])
    pooled = pool_line[0]
    for line in range(1, lines):
        pooled = pooled + pool_line[line]
    pooled = pooled * (1.0 / (rows * pixels))
    pooled = jax.nn.relu(pooled + branch_bias_ref[4:5, :]).astype(BF16)
    constant = jnp.dot(pooled, proj_ref[4 * width :, :], preferred_element_type=F32)
    constant = constant[0:1, :] + proj_bias_ref[...]

    project(two + 1, False)
    finish_level(three)
    project(three + 1, False)

    value = jax.nn.relu(total[...] + constant).astype(BF16).reshape(strip, window, width)
    context[...] = value
    out_ref[1 : strip + 1] = value
    for at, (row, offset) in enumerate(((0, -1), (strip - 1, 1))):
        cond = (me + offset >= 0) & (me + offset < rows)
        send(
            cond,
            remote(context.at[row], halo.at[at], halo_ssem.at[at], halo_rsem.at[at], {"rows": me + offset}),
        )
    for at, (row, offset) in enumerate(((0, -1), (strip - 1, 1))):
        place = strip + 1 if at == 0 else 0
        edge = strip - 1 if at == 0 else 0
        cond = (me - offset >= 0) & (me - offset < rows)
        arrive(cond, halo.at[at], halo_rsem.at[at], halo_ssem.at[at])

        @pl.when(cond)
        def _():
            out_ref[place] = halo[at]

        @pl.when(jnp.logical_not(cond))
        def _():
            out_ref[place] = context[edge]

    for cond, copy in pending:
        if cond is None:
            copy.wait_send()
        else:
            pl.when(cond)(copy.wait_send)


def pyramid(features, w_one, w_rate, w_pool, b_branch, w_proj, b_proj, low_features, w_low, b_low):
    strip, cols, depth = features.shape
    levels, taps, shard = w_rate.shape[0], w_rate.shape[1], w_rate.shape[3]
    width = w_one.shape[1]
    rows = lax.axis_size("rows")
    lines = rows // 4
    window = cols // 2 + 16
    pixels = strip * cols
    own = jnp.swapaxes(w_rate, 2, 3)
    sources = lines // 2
    fine_rows, fine_cols, low_depth = low_features.shape
    low_width = w_low.shape[1]
    packed = pl.cdiv(3 * low_width, 128) * 128
    rest = packed - 3 * low_width
    low_weight = jnp.pad(jnp.concatenate([w_low] * 3, axis=1), ((0, 0), (0, rest)))
    low_bias = jnp.pad(jnp.concatenate([b_low] * 3), (0, rest))[None, :]
    dma = pltpu.SemaphoreType.DMA
    vmem = pl.BlockSpec(memory_space=pltpu.VMEM)
    return pl.pallas_call(
        lambda *refs: pyramid_kernel((rows, lines, window, low_width), *refs),
        out_shape=(
            jax.ShapeDtypeStruct((strip + 2, window, width), BF16),
            jax.ShapeDtypeStruct((fine_rows + 2, fine_cols, packed), BF16),
        ),
        in_specs=[vmem] * 10,
        out_specs=(vmem, vmem),
        scratch_shapes=[
            pltpu.VMEM((rows // 2, levels, taps, shard, depth), BF16),
            pltpu.VMEM((2, strip, cols, depth), BF16),
            pltpu.VMEM((levels, 2, 2, strip, cols, depth), BF16),
            pltpu.VMEM((levels, 2, 3, strip, cols, width // 2), BF16),
            pltpu.VMEM((levels, 3, strip, cols, width), BF16),
            pltpu.VMEM((levels + 1, strip, cols, width), BF16),
            pltpu.VMEM((levels + 1, strip, window, width), BF16),
            pltpu.VMEM((strip * window, width), F32),
            pltpu.VMEM((strip, window, width), BF16),
            pltpu.VMEM((2, window, width), BF16),
            pltpu.VMEM((4, 8, width), F32),
            pltpu.VMEM((3, 8, width), F32),
            pltpu.VMEM((lines, 8, width), F32),
            dma((levels, sources)),
            dma((levels, 3 * sources)),
            dma((levels, rows // 2)),
            dma((levels, 5, 2)),
            dma((levels, 5, 2)),
            dma((levels + 1,)),
            dma((levels + 1,)),
            dma((2,)),
            dma((2,)),
            dma((3 + 2 * lines,)),
            dma((3 + lines,)),
            dma,
            dma,
            pltpu.VMEM((fine_rows, low_depth), F32),
            pltpu.VMEM((fine_rows, packed), F32),
            pltpu.VMEM((fine_rows, packed), F32),
            pltpu.VMEM((2, fine_cols, packed), BF16),
            pltpu.VMEM((2, fine_cols, packed), BF16),
            dma((3,)),
            dma((3,)),
        ],
        compiler_params=pltpu.CompilerParams(
            collective_id=0, has_side_effects=True, vmem_limit_bytes=56 * 1024 * 1024
        ),
        cost_estimate=pl.CostEstimate(
            flops=2 * pixels * depth * width * (levels * taps + 1),
            bytes_accessed=2 * levels * taps * depth * width,
            transcendentals=0,
        ),
    )(
        features, own, w_one, w_pool, b_branch, w_proj, b_proj[None, :],
        low_features, low_weight, low_bias,
    )


def decoder_kernel(
    strip, coarse_ref, low_ref, blend_ref, up_weight_ref, low_weight_ref, bias_ref, out_ref, fine
):
    at = pl.program_id(0)
    me = lax.axis_index("rows")
    rows = lax.axis_size("rows")
    block, fine_cols, width = out_ref.shape
    fine_rows = fine.shape[0] - 2
    window, depth = coarse_ref.shape[1], coarse_ref.shape[2]

    @pl.when(at == 0)
    def _():
        for row in range(fine_rows + 2):
            pair, phase = divmod(row + 1, 4)
            source = coarse_ref[pair : pair + 2].reshape(2 * window, depth)
            for across in range(3):
                value = jnp.dot(
                    blend_ref[phase, across * fine_cols : (across + 1) * fine_cols, :],
                    source,
                    preferred_element_type=F32,
                )
                if row == 0:
                    value = jnp.where(me == 0, 0.0, value)
                if row == fine_rows + 1:
                    value = jnp.where(me == rows - 1, 0.0, value)
                fine[row, :, across * depth : (across + 1) * depth] = value.astype(BF16)

    total = None
    for down in range(3):
        up = fine[pl.ds(at * block + down, block)].reshape(block * fine_cols, 3 * depth)
        low = low_ref[pl.ds(at * block + down, block)].reshape(block * fine_cols, low_ref.shape[2])
        term = jnp.dot(up, up_weight_ref[down], preferred_element_type=F32)
        term = term + jnp.dot(low, low_weight_ref[down], preferred_element_type=F32)
        total = term if total is None else total + term
    total = jax.nn.relu(total + bias_ref[...])
    out_ref[...] = total.astype(BF16).reshape(block, fine_cols, width)


def blend_matrices(half, window, chan_index):
    fine_cols = 4 * half
    shape = (4, 3, fine_cols, 2, window)
    phase, across, pos, lower, col = (lax.broadcasted_iota(jnp.int32, shape, d) for d in range(5))
    place = pos + across - 1
    pair, col_phase = (place + 2) // 4, (place + 2) % 4
    first = jnp.clip(chan_index * half + pair - 1, 0, 2 * half - 1) - chan_index * (2 * half - window)
    second = jnp.clip(chan_index * half + pair, 0, 2 * half - 1) - chan_index * (2 * half - window)
    col_upper = 0.875 - 0.25 * col_phase.astype(F32)
    factor = jnp.where(col == first, col_upper, 0.0) + jnp.where(col == second, 1.0 - col_upper, 0.0)
    row_upper = 0.875 - 0.25 * phase.astype(F32)
    factor = factor * jnp.where(lower == 0, row_upper, 1.0 - row_upper)
    whole = chan_index * fine_cols + place
    factor = jnp.where((whole >= 0) & (whole < 2 * fine_cols), factor, 0.0)
    return factor.astype(BF16).reshape(4, 3 * fine_cols, 2 * window)


def whole_by_kernels(
    features, low_features, w_one, w_rate, w_pool, b_branch, w_proj, b_proj, w_low, b_low,
    w_dec_up, w_dec_low, b_dec,
):
    strip, cols = features.shape[0], features.shape[1]
    fine_rows, fine_cols = low_features.shape[0], low_features.shape[1]
    depth, width = w_dec_up.shape[1], w_dec_up.shape[2]
    chan_index = lax.axis_index("chan")
    half = cols // 2
    padded, low_packed = pyramid(
        features, w_one, w_rate, w_pool, b_branch, w_proj, b_proj, low_features, w_low, b_low
    )
    window, packed = padded.shape[1], low_packed.shape[2]
    context = jnp.where(chan_index == 0, padded[1:-1, :half], padded[1:-1, window - half :])
    up_weight = w_dec_up.reshape(3, 3 * depth, width)
    low_weight = w_dec_low.reshape(3, -1, width)
    low_weight = jnp.pad(low_weight, ((0, 0), (0, packed - low_weight.shape[1]), (0, 0)))
    blend = blend_matrices(half, window, chan_index)
    whole = pl.BlockSpec(memory_space=pltpu.VMEM)
    block = 4
    pixels = fine_rows * fine_cols
    decoded = pl.pallas_call(
        lambda *refs: decoder_kernel(strip, *refs),
        out_shape=jax.ShapeDtypeStruct((fine_rows, fine_cols, width), BF16),
        grid=(fine_rows // block,),
        in_specs=[whole] * 6,
        out_specs=pl.BlockSpec((block, fine_cols, width), lambda i: (i, 0, 0)),
        scratch_shapes=[pltpu.VMEM((fine_rows + 2, fine_cols, 3 * depth), BF16)],
        compiler_params=pltpu.CompilerParams(vmem_limit_bytes=48 * 1024 * 1024),
        cost_estimate=pl.CostEstimate(
            flops=2 * pixels * width * (9 * depth + 3 * packed),
            bytes_accessed=2 * pixels * (width + packed),
            transcendentals=0,
        ),
    )(padded, low_packed, blend, up_weight, low_weight, b_dec[None, :])
    return context, decoded


def context_by_collectives(features, w_one, w_rate, w_pool, b_branch, w_proj, b_proj):
    strip_rows, map_cols, group_in = features.shape
    branch_width = w_one.shape[1]
    pixel_count = strip_rows * map_cols
    rows_index = lax.axis_index("rows")
    rows_count = lax.axis_size("rows")
    chan_index = lax.axis_index("chan")
    chan_count = lax.axis_size("chan")
    local_sum = jnp.sum(features, axis=(0, 1), dtype=jnp.float32)
    map_total = strip_rows * rows_count * map_cols
    pool_weight = w_pool.astype(jnp.float32)
    pooled = lax.psum(local_sum, "rows") / map_total
    local_term = jnp.dot(pooled, pool_weight, precision=lax.Precision.HIGHEST)
    pool_pre = lax.psum(local_term, "chan")
    pool_branch = jax.nn.relu(pool_pre + b_branch[4]).astype(jnp.bfloat16)
    head_weight = w_proj[: 4 * branch_width]
    pool_term = jnp.dot(
        pool_branch[None, :], w_proj[4 * branch_width :], preferred_element_type=jnp.float32
    )[0]
    rate_all = lax.all_gather(w_rate, "rows", axis=3, tiled=True)
    rate_outputs = []
    for rate_level in range(3):
        matrix = rate_matrix(features, RATE * (rate_level + 1))
        weight_flat = rate_all[rate_level].reshape(-1, rate_all.shape[3])
        rate_outputs.append(jnp.dot(matrix, weight_flat, preferred_element_type=jnp.float32))
    one_out = jnp.dot(
        features.reshape(pixel_count, group_in), w_one, preferred_element_type=jnp.float32
    )
    partial_value = jnp.concatenate([one_out] + rate_outputs, axis=1).reshape(
        strip_rows, map_cols, 4 * branch_width
    )
    conv_bias = b_branch[:4].reshape(-1)
    summed = lax.psum_scatter(
        partial_value.astype(jnp.bfloat16), "chan", scatter_dimension=2, tiled=True
    ).astype(jnp.float32)
    share_width = summed.shape[2]
    bias_share = lax.dynamic_slice_in_dim(conv_bias, chan_index * share_width, share_width)
    branches = jax.nn.relu(summed + bias_share).astype(jnp.bfloat16)
    weight_share = lax.dynamic_slice_in_dim(head_weight, chan_index * share_width, share_width, 0)
    partial_terms = jnp.dot(
        branches.reshape(-1, share_width), weight_share, preferred_element_type=jnp.float32
    )
    partial_terms = partial_terms.reshape(strip_rows, map_cols, branch_width)
    projected = lax.psum_scatter(
        partial_terms.astype(jnp.bfloat16), "chan", scatter_dimension=1, tiled=True
    ).astype(jnp.float32)
    context = jax.nn.relu(projected + pool_term + b_proj).astype(jnp.bfloat16)
    coarse = padded_2(context, (("rows", 0), ("chan", 1)), 1)
    coarse = edge_copy(coarse, rows_index, rows_count, chan_index, chan_count)
    return context, coarse


def on_device(
    features,
    low_features,
    w_one,
    w_rate,
    w_pool,
    b_branch,
    w_proj,
    b_proj,
    w_low,
    b_low,
    w_dec_up,
    w_dec_low,
    b_dec,
):
    rows_index = lax.axis_index("rows")
    rows_count = lax.axis_size("rows")
    chan_index = lax.axis_index("chan")
    chan_count = lax.axis_size("chan")
    fits = (
        chan_count == 2
        and rows_count % 8 == 0
        and w_one.shape[1] % 256 == 0
        and w_rate.shape[3] % 16 == 0
        and features.shape[1] % 32 == 0
        and features.shape[2] % 128 == 0
        and features.shape[0] % 2 == 0
        and low_features.shape[0] == 4 * features.shape[0]
        and low_features.shape[0] % 16 == 0
        and 2 * low_features.shape[1] == 4 * features.shape[1]
    )
    if fits:
        return whole_by_kernels(
            features, low_features, w_one, w_rate, w_pool, b_branch, w_proj, b_proj, w_low, b_low,
            w_dec_up, w_dec_low, b_dec,
        )
    context, coarse = context_by_collectives(
        features, w_one, w_rate, w_pool, b_branch, w_proj, b_proj
    )
    tile_rows_count = context.shape[0]
    tile_cols_count = context.shape[1]
    fine_rows, fine_cols = (low_features.shape[0], low_features.shape[1])
    low_flat = low_features.reshape(fine_rows * fine_cols, low_features.shape[2])
    low_mapped = jax.nn.relu(
        jnp.dot(low_flat, w_low, preferred_element_type=jnp.float32) + b_low
    ).astype(jnp.bfloat16)
    low_mapped = low_mapped.reshape(fine_rows, fine_cols, -1)
    coarse = coarse.astype(jnp.float32)
    upsampled = blend_axis(coarse, 0)[1 : 4 * tile_rows_count + 3]
    upsampled = blend_axis(upsampled, 1)[:, 1 : 4 * tile_cols_count + 3]
    ext_rows, ext_cols = (upsampled.shape[0], upsampled.shape[1])
    row_pos = lax.broadcasted_iota(jnp.int32, (ext_rows, 1, 1), 0)
    col_pos = lax.broadcasted_iota(jnp.int32, (1, ext_cols, 1), 1)
    inside = ((row_pos > 0) | (rows_index > 0)) & (
        (row_pos < ext_rows - 1) | (rows_index < rows_count - 1)
    )
    inside = (
        inside
        & ((col_pos > 0) | (chan_index > 0))
        & ((col_pos < ext_cols - 1) | (chan_index < chan_count - 1))
    )
    up_pad = jnp.where(inside, upsampled, 0.0).astype(jnp.bfloat16)
    low_pad = padded_2(low_mapped, (("rows", 0), ("chan", 1)), 1)
    up_taps = tap_matrix(up_pad, fine_rows, fine_cols)
    low_taps = tap_matrix(low_pad, fine_rows, fine_cols)
    mixed = jnp.dot(
        up_taps, w_dec_up.reshape(-1, w_dec_up.shape[2]), preferred_element_type=jnp.float32
    )
    mixed = mixed + jnp.dot(
        low_taps, w_dec_low.reshape(-1, w_dec_low.shape[2]), preferred_element_type=jnp.float32
    )
    decoded = jax.nn.relu(mixed + b_dec).astype(jnp.bfloat16).reshape(fine_rows, fine_cols, -1)
    return (context, decoded)


def solution(mesh):
    in_specs = (
        P("rows", None, "chan"),
        P("rows", "chan", None),
        P("chan", None),
        P(None, None, "chan", "rows"),
        P("chan", None),
        P(),
        P(),
        P(),
        P(),
        P(),
        P(),
        P(),
        P(),
    )
    out_specs = (P("rows", "chan", None), P("rows", "chan", None))
    return jax.shard_map(
        on_device, mesh=mesh, in_specs=in_specs, out_specs=out_specs, check_vma=False
    )
```
